32 devices in a mesh: gx: 8 (over z, y), gy: 4 (over x, core).
Axes of the slice: x: 2, y: 2, z: 4, core: 2. Of those that a mesh axis runs over, the one named last changes fastest.
Arguments:
- cell_means: float32 [30, 32, 16, 128], P(None, 'gx', 'gy'), may hold values from 0 to 1
- diffusion: float32 [32, 16, 128], P('gx', 'gy'), may hold values from 0.02 to 0.15
- mix_rate: float32 [32, 16, 128], P('gx', 'gy'), may hold values from 0.05 to 3
- send_lists: int32 [32, 32, 128], P(('gx', 'gy')), may hold values from 0 to 2047
- compositions: float32 [30, 131072], P(None, ('gx', 'gy')), may hold values from 0 to 1
- weights: float32 [131072], P(('gx', 'gy')), may hold values from 0.5 to 2
- particle_slots: int32 [131072], P(('gx', 'gy')), may hold values from 0 to 4095
- partners: int32 [131072], P(('gx', 'gy')), may hold values from 0 to 4095
Outputs:
- new_means: float32 [30, 32, 16, 128], P(None, 'gx', 'gy')
- new_compositions: float32 [30, 131072], P(None, ('gx', 'gy'))
The draws below stay inside these ranges and needn't reach their ends.
Inputs may be any that keep to these rules, and one draw needn't show every extreme that they name: particle_slots = s * 128 + r names slot r of the list that tile s sends to the particle's device.
All inputs are finite; a program needn't handle non-finite values.
Results may differ from the reference program's by a relative error of at most 0.00002.
Values sent between devices are 32-bit elements; how exact they have to be, the bound alone decides.
A program may use at most 64 MiB of HBM per device.

```python
import math
import jax
import jax.numpy as jnp
import numpy as np

SPECIES = 30
CX = 4
CY = 4
CZ = 128
SLOTS = 128
P_DEV = 4096
NX = 32
NY = 16
PARTS_SIZE = 131072
N_GX = 8
N_GY = 4


def place_ends(drawn, own_key, smallest, largest):
    longest = drawn.shape.index(max(drawn.shape))
    spots = []
    for shift in (0, 1):
        where = [jax.random.randint(jax.random.fold_in(own_key, axis), (), 0, length) for axis, length in enumerate(drawn.shape)]
        where[longest] = (where[longest] + shift) % drawn.shape[longest]
        spots.append(tuple(where))
    return drawn.at[spots[0]].set(smallest).at[spots[1]].set(largest)


def block_scale(stream_key, shape, shards, low, largest):
    factor_of = 1.0
    for axis_at, shards_of in shards:
        steps = jax.random.uniform(jax.random.fold_in(jax.random.fold_in(stream_key, 6), axis_at), (shards_of,), jnp.float32, low / len(shards), largest / len(shards))
        factor_of = factor_of * jnp.repeat(jnp.exp(steps), shape[axis_at] // shards_of).reshape((-1,) + (1,) * (len(shape) - 1 - axis_at))
    return factor_of


def rank_bounds(amount, skew):
    loads = [(1 << 20) // math.isqrt(grade ** skew) + 1 for grade in range(1, amount + 1)]
    deviation = 1 + sum(loads) // (1 << 30)
    return np.cumsum(np.array([max(1, weight // deviation) for weight in loads]))


def ranked_ids(key, extent, number_of, skew):
    listing = rank_bounds(number_of, skew)
    ticket = jax.random.randint(jax.random.fold_in(key, 1), extent, 0, int(listing[number_of - 1]))
    rank = jnp.searchsorted(jnp.asarray(listing, jnp.int32), ticket, side="right")
    return jax.random.permutation(jax.random.fold_in(key, 2), number_of)[rank].astype(jnp.int32)


def setup_inputs(seed: int = 0) -> dict:
    keys = jax.random.split(jax.random.key(seed), 9)
    return {
        "cell_means": jnp.clip(1.0 * jax.random.uniform(keys[0], (SPECIES, NX, NY, CZ), jnp.float32) ** block_scale(keys[0], (SPECIES, NX, NY, CZ), ((1, 8), (2, 4)), -0.2, 0.2), 0.0, 1.0),
        "diffusion": jnp.clip(0.02 + 0.13000001 * jax.random.uniform(keys[1], (NX, NY, CZ), jnp.float32) ** block_scale(keys[1], (NX, NY, CZ), ((0, 8), (1, 4)), -0.2, 0.2), 0.02, 0.15),
        "mix_rate": jnp.clip(jnp.exp(math.log(3.0) - 4.0943445 * jax.random.uniform(keys[2], (NX, NY, CZ), jnp.float32) ** block_scale(keys[2], (NX, NY, CZ), ((0, 8), (1, 4)), -0.2, 0.2)), 0.05, 3.0),
        "send_lists": place_ends(jax.random.randint(keys[3], (N_GX * N_GY, N_GX * N_GY, SLOTS), 0, CX * CY * CZ), jax.random.fold_in(keys[3], 1), 0, (CX * CY * CZ) - 1).astype(jnp.int32),
        "compositions": jnp.clip(1.0 * jax.random.uniform(keys[4], (SPECIES, PARTS_SIZE), jnp.float32) ** block_scale(keys[4], (SPECIES, PARTS_SIZE), ((1, 32),), -0.2, 0.2), 0.0, 1.0),
        "weights": jnp.clip(jnp.exp(math.log(2.0) - 1.3862944 * jax.random.uniform(keys[5], (PARTS_SIZE,), jnp.float32) ** block_scale(keys[5], (PARTS_SIZE,), ((0, 32),), -0.2, 0.2)), 0.5, 2.0),
        "particle_slots": place_ends(ranked_ids(keys[6], (PARTS_SIZE,), N_GX * N_GY * SLOTS, 1), jax.random.fold_in(keys[6], 3), 0, (N_GX * N_GY * SLOTS) - 1).astype(jnp.int32),
        "partners": place_ends(jax.random.randint(keys[7], (PARTS_SIZE,), 0, P_DEV), jax.random.fold_in(keys[7], 1), 0, P_DEV - 1).astype(jnp.int32),
    }


PAIR_RATE = 0.3


def reference(cell_means, diffusion, mix_rate, send_lists, compositions, weights, particle_slots, partners):
    devices = N_GX * N_GY
    cell_count = CX * CY * CZ
    padded = jnp.pad(cell_means, ((0, 0), (1, 1), (1, 1), (1, 1)))
    neighbours = padded[:, 2:, 1:-1, 1:-1] + padded[:, :-2, 1:-1, 1:-1]
    neighbours = neighbours + padded[:, 1:-1, 2:, 1:-1] + padded[:, 1:-1, :-2, 1:-1]
    neighbours = neighbours + padded[:, 1:-1, 1:-1, 2:] + padded[:, 1:-1, 1:-1, :-2]
    filtered = cell_means + diffusion[None] * (neighbours - 6.0 * cell_means)
    fields = jnp.concatenate([filtered, mix_rate[None]], 0)
    blocks = fields.reshape(SPECIES + 1, N_GX, CX, N_GY, CY, CZ).transpose(1, 3, 2, 4, 5, 0)
    blocks = blocks.reshape(devices * cell_count, SPECIES + 1)
    owner = (jnp.arange(devices * P_DEV) // P_DEV).astype(jnp.int32)
    source = (particle_slots // SLOTS).astype(jnp.int32)
    within = (particle_slots % SLOTS).astype(jnp.int32)
    target = source * cell_count + send_lists[source, owner, within]
    local_means = blocks[target].T
    blend_rate = 1.0 - jnp.exp(-local_means[SPECIES])
    mates = compositions[:, owner * P_DEV + partners]
    new_compositions = compositions - blend_rate[None] * (compositions - local_means[:SPECIES]) - PAIR_RATE * (compositions - mates)
    weighted = jnp.concatenate([weights[None] * new_compositions, weights[None]], 0)
    totals = jax.ops.segment_sum(weighted.T, target, num_segments=devices * cell_count)
    updated = (totals[:, :SPECIES] + blocks[:, :SPECIES]) / (totals[:, SPECIES:] + 1.0)
    new_means = updated.reshape(N_GX, N_GY, CX, CY, CZ, SPECIES).transpose(5, 0, 2, 1, 3, 4)
    new_means = new_means.reshape(SPECIES, NX, NY, CZ)
    return new_means, new_compositions
```

```python
import functools

import jax
import jax.numpy as jnp
from jax import lax
from jax.experimental import pallas as pl
from jax.experimental.pallas import tpu as pltpu
from jax.sharding import PartitionSpec as P

PAIR_RATE = 0.3
LANES = 128
ROWS = 32
GROUPS = ROWS // 8
PLANE = 8
F32 = jnp.float32
BF16 = jnp.bfloat16


def pick(table, count, index, start=0, sums=None):
    lane = jnp.broadcast_to(index & (LANES - 1), (8, LANES))
    chunk = jnp.broadcast_to(index >> 7, (8, LANES))
    if sums is None:
        sums = tuple(jnp.zeros((8, LANES), F32) for _ in range(GROUPS))

    def step(at, sums):
        mask = chunk == at
        return tuple(
            jnp.where(
                mask,
                jnp.take_along_axis(
                    table[at, 8 * g : 8 * g + 8, :], lane, axis=1, mode="promise_in_bounds"
                ),
                total,
            )
            for g, total in enumerate(sums)
        )

    return lax.fori_loop(start, start + count, step, sums, unroll=min(count, 16))


def stencil(cells, halo, diffusion, fields, rows_x, rows_y):
    lane = lax.broadcasted_iota(jnp.int32, (ROWS, LANES), 1)
    for x in range(rows_x):
        for y in range(rows_y):
            mid = cells[x, y]
            total = cells[x + 1, y] if x + 1 < rows_x else halo[1, y]
            total = total + (cells[x - 1, y] if x else halo[0, y])
            total = total + (cells[x, y + 1] if y + 1 < rows_y else halo[3, x])
            total = total + (cells[x, y - 1] if y else halo[2, x])
            total = total + jnp.where(lane < LANES - 1, pltpu.roll(mid, LANES - 1, 1), 0.0)
            total = total + jnp.where(lane > 0, pltpu.roll(mid, 1, 1), 0.0)
            j = x * rows_y + y
            fields[j] = mid + diffusion[j : j + 1, :] * (total - 6.0 * mid)


def scatter_block(group, hot, high, low, left, acc, groups):
    width = group.shape[1]
    group = jnp.broadcast_to(group.astype(F32).astype(BF16), (ROWS, width))
    for g in range(groups):
        mask = group == jnp.array(g, BF16)
        zero = jnp.zeros((ROWS, width), BF16)
        left[2 * g * ROWS : (2 * g + 1) * ROWS, :] = jnp.where(mask, high, zero)
        left[(2 * g + 1) * ROWS : (2 * g + 2) * ROWS, :] = jnp.where(mask, low, zero)
    acc[...] += lax.dot_general(
        left[...], hot, (((1,), (1,)), ((), ())), preferred_element_type=F32
    )


def hot_rows(index):
    place = lax.broadcasted_iota(jnp.int32, (256, index.shape[1]), 0)
    return jnp.where(place == (index & 255), 1.0, 0.0).astype(BF16)


def acc_row(acc, j):
    g, half = j // 2, (j % 2) * LANES
    return (
        acc[2 * g * ROWS : (2 * g + 1) * ROWS, half : half + LANES]
        + acc[(2 * g + 1) * ROWS : (2 * g + 2) * ROWS, half : half + LANES]
    )


def load_cells(means, cells, rows_x, rows_y):
    species = means.shape[0] // (rows_x * rows_y)
    for x in range(rows_x):
        for y in range(rows_y):
            j = x * rows_y + y
            cells[x, y, 0:species, :] = means[pl.ds(j, species, stride=rows_x * rows_y), :]
            cells[x, y, species:ROWS, :] = jnp.zeros((ROWS - species, LANES), F32)


def gather_pairs(compositions, partners, table, parts, pair):
    species, particles = compositions.shape
    groups = particles // 256
    for h in range(groups):
        values = compositions[:, h * 256 : (h + 1) * 256]
        values = jnp.concatenate([values, jnp.zeros((ROWS - species, 256), F32)], 0)
        first = values.astype(BF16)
        table[h * ROWS : (h + 1) * ROWS, 0:256] = first
        table[h * ROWS : (h + 1) * ROWS, 256:512] = (values - first.astype(F32)).astype(BF16)

    def body(k, _):
        index = jnp.concatenate([partners[pl.ds(2 * k + i, 1), :] for i in range(2)], 1)
        place = lax.broadcasted_iota(jnp.int32, (256, 256), 0)
        hot = jnp.where(place == (index & 255), 1.0, 0.0).astype(BF16)
        hot = jnp.concatenate([hot, hot], 0)
        parts[...] = jnp.dot(table[...], hot, preferred_element_type=F32)
        group = jnp.broadcast_to(index >> 8, (ROWS, 256))
        total = jnp.zeros((ROWS, 256), F32)
        for h in range(groups):
            total = jnp.where(group == h, parts[h * ROWS : (h + 1) * ROWS, :], total)
        at = pl.multiple_of(k * 256, 256)
        pair[0:species, pl.ds(at, 256)] = PAIR_RATE * (
            compositions[:, pl.ds(at, 256)] - total[:species]
        )
        return 0

    lax.fori_loop(0, particles // 256, body, 0)


def pick_rates(lists, rates, buffer):
    tiles = lists.shape[0]
    for first in range(0, tiles, 8):
        index = lists[first : first + 8, :]
        lane, chunk = index & (LANES - 1), index >> 7
        total = jnp.zeros((8, LANES), F32)
        for j in range(rates.shape[0]):
            row = jnp.broadcast_to(rates[j : j + 1, :], (8, LANES))
            found = jnp.take_along_axis(row, lane, axis=1, mode="promise_in_bounds")
            total = jnp.where(chunk == j, found, total)
        for i in range(8):
            buffer[first + i] = total[i : i + 1, :]


def spread_rates(slots, rates, out):
    blocks = slots.shape[0]
    parts = range(0, blocks, 8)
    lanes = [slots[b : b + 8, :] & (LANES - 1) for b in parts]
    chunks = [slots[b : b + 8, :] >> 7 for b in parts]

    def step(s, totals):
        row = jnp.broadcast_to(rates[s], (8, LANES))
        return tuple(
            jnp.where(
                chunk == s,
                jnp.take_along_axis(row, lane, axis=1, mode="promise_in_bounds"),
                total,
            )
            for lane, chunk, total in zip(lanes, chunks, totals)
        )

    start = tuple(jnp.zeros((8, LANES), F32) for _ in parts)
    totals = lax.fori_loop(0, rates.shape[0], step, start, unroll=8)
    for b, total in zip(parts, totals):
        out[b : b + 8, :] = total


def add_fields(received, slots, hot, table, parts, new):
    species, particles = new.shape
    groups = received.shape[0] // 2

    def fill(h, _):
        values = jnp.concatenate([received[2 * h], received[2 * h + 1]], 1)
        first = values.astype(BF16)
        at = pl.ds(pl.multiple_of(h * ROWS, ROWS), ROWS)
        table[at, 0:256] = first
        table[at, 256:512] = (values - first.astype(F32)).astype(BF16)
        return 0

    lax.fori_loop(0, groups, fill, 0)

    def body(k, _):
        at = pl.ds(pl.multiple_of(k * 256, 256), 256)
        both = hot[:, at]
        both = jnp.concatenate([both, both], 0)
        parts[...] = jnp.dot(table[...], both, preferred_element_type=F32)
        index = jnp.concatenate([slots[pl.ds(2 * k + i, 1), :] for i in range(2)], 1)
        group = jnp.broadcast_to(index >> 8, (ROWS, 256))
        total = jnp.zeros((ROWS, 256), F32)
        for h in range(groups):
            total = jnp.where(group == h, parts[h * ROWS : (h + 1) * ROWS, :], total)
        new[:, at] += total[:species]
        return 0

    lax.fori_loop(0, particles // 256, body, 0)


def whole_kernel(
    nx, ny, rows_x, rows_y, *refs
):
    inputs, (out, new), refs = refs[:8], refs[8:10], refs[10:]
    staged, refs = refs[:8], refs[8:]
    means, diffusion, rate, lists, compositions, weights, slots, partners = staged
    (
        cells, halo, fields, scaled, rates_out, rates_in, rates, outgoing, received, moments,
        returned, table, parts, pair, high, low, hot1, left1, acc1, field_table, field_parts,
        left2, acc2,
        in_sems, halo_send, halo_recv, rate_send, rate_recv, go_send, go_recv,
        back_send, back_recv,
    ) = refs
    tiles = nx * ny
    planes = tiles // PLANE
    count = rows_x * rows_y
    species = compositions.shape[0]
    blocks = slots.shape[0]
    gx, gy = lax.axis_index("gx"), lax.axis_index("gy")
    me = gx * ny + gy
    plane, inner = lax.div(me, PLANE), lax.rem(me, PLANE)

    def place(d):
        return (lax.div(d, ny), lax.rem(d, ny))

    loads = [
        pltpu.make_async_copy(inputs[i], staged[i], in_sems.at[i]) for i in range(8)
    ]
    for i in (2, 3, 0, 1, 6, 4, 7, 5):
        loads[i].start()

    barrier = pltpu.get_barrier_semaphore()

    def greet(k, _):
        d = lax.rem(me + k, tiles)
        pl.semaphore_signal(
            barrier, inc=1, device_id=place(d), device_id_type=pl.DeviceIdType.MESH
        )
        return 0

    lax.fori_loop(1, tiles, greet, 0)

    loads[2].wait()
    loads[3].wait()
    blend = 1.0 - jnp.exp(-rate[...])
    pick_rates(lists, blend, rates_out)
    loads[0].wait()
    for x in range(rows_x):
        for y in range(rows_y):
            j = x * rows_y + y
            cells[x, y, 0:species, :] = means[pl.ds(j, species, stride=count), :]
            cells[x, y, species:ROWS, :] = jnp.zeros((ROWS - species, LANES), F32)
    rates_in[me] = rates_out[me]

    pl.semaphore_wait(barrier, tiles - 1)

    def halo_copy(i):
        source, length, target = (
            (cells.at[rows_x - 1], rows_y, (gx + 1, gy)),
            (cells.at[0], rows_y, (gx - 1, gy)),
            (cells.at[:, rows_y - 1], rows_x, (gx, gy + 1)),
            (cells.at[:, 0], rows_x, (gx, gy - 1)),
        )[i]
        return pltpu.make_async_remote_copy(
            src_ref=source,
            dst_ref=halo.at[i, 0:length],
            send_sem=halo_send.at[i],
            recv_sem=halo_recv.at[i],
            device_id=target,
            device_id_type=pl.DeviceIdType.MESH,
        )

    sends = (gx < nx - 1, gx > 0, gy < ny - 1, gy > 0)
    receives = (gx > 0, gx < nx - 1, gy > 0, gy < ny - 1)
    for i in range(4):

        @pl.when(sends[i])
        def _(i=i):
            halo_copy(i).start()

        @pl.when(jnp.logical_not(receives[i]))
        def _(i=i):
            halo[i] = jnp.zeros(halo.shape[1:], F32)

    def rate_copy(source, d, target):
        return pltpu.make_async_remote_copy(
            src_ref=rates_out.at[d],
            dst_ref=rates_in.at[source],
            send_sem=rate_send.at[d],
            recv_sem=rate_recv.at[source],
            device_id=place(target),
            device_id_type=pl.DeviceIdType.MESH,
        )

    def send_rates(k, _):
        d = lax.rem(me + k, tiles)
        rate_copy(me, d, d).start()
        return 0

    lax.fori_loop(1, tiles, send_rates, 0)

    loads[6].wait()
    for b in range(0, blocks, 4):
        index = jnp.concatenate([slots[b + i : b + i + 1, :] for i in range(4)], 1)
        hot1[:, b * LANES : (b + 4) * LANES] = hot_rows(index)
    loads[1].wait()

    for i in range(4):

        @pl.when(receives[i])
        def _(i=i):
            halo_copy(i).wait_recv()

    stencil(cells, halo, diffusion, fields, rows_x, rows_y)

    def copy_of(buffers, sems, rows, source, d, target):
        return pltpu.make_async_remote_copy(
            src_ref=buffers[0].at[d, 0:rows],
            dst_ref=buffers[1].at[source, 0:rows],
            send_sem=sems[0].at[d],
            recv_sem=sems[1].at[source],
            device_id=place(target),
            device_id_type=pl.DeviceIdType.MESH,
        )

    go = (outgoing, received), (go_send, go_recv), species
    back = (moments, returned), (back_send, back_recv), species + 1

    for j in range(count):
        scaled[j] = fields[j] * blend[j : j + 1, :]

    def fill(d, buffer, row):
        found = pick(scaled, count, lists[pl.ds(d, 1), :])
        for g in range(GROUPS):
            buffer[row, 8 * g : 8 * g + 8, :] = found[g]

    def send_plane(there, first):
        def body(i, _):
            d = there * PLANE + lax.rem(inner + i, PLANE)
            fill(d, outgoing, d)
            copy_of(*go, me, d, d).start()
            return 0

        lax.fori_loop(first, PLANE, body, 0)

    def far_first(step):
        half = planes // 2
        lax.fori_loop(half, planes, lambda k, _: (step(k), 0)[1], 0)
        lax.fori_loop(1, half, lambda k, _: (step(half - k), 0)[1], 0)

    far_first(lambda k: send_plane(lax.rem(plane + k, planes), 0))
    fill(me, received, me)
    send_plane(plane, 1)

    loads[4].wait()
    loads[7].wait()
    gather_pairs(compositions, partners, table, parts, pair)
    loads[5].wait()

    def wait_rates(k, _):
        s = lax.rem(me + k, tiles)
        rate_copy(s, s, s).wait_recv()
        return 0

    lax.fori_loop(1, tiles, wait_rates, 0)
    spread_rates(slots, rates_in, rates)

    def weigh(b, _):
        at = pl.ds(pl.multiple_of(b * LANES, LANES), LANES)
        mine = compositions[:, at]
        fresh = mine - rates[pl.ds(b, 1), :] * mine - pair[0:species, at]
        new[:, at] = fresh
        weight = weights[pl.ds(b, 1), :]
        values = jnp.concatenate(
            [weight * fresh, weight, jnp.zeros((ROWS - species - 1, LANES), F32)], 0
        )
        top = values.astype(BF16)
        high[:, at] = top
        low[:, at] = (values - top.astype(F32)).astype(BF16)
        return 0

    lax.fori_loop(0, blocks, weigh, 0, unroll=4)

    per = left1.shape[1]
    wide = acc1.shape[0] // ROWS

    def sum_slots(part, last):
        acc1[...] = jnp.zeros(acc1.shape, F32)

        def scatter(k, _):
            rows = [slots[pl.ds(k * (per // LANES) + i, 1), :] for i in range(per // LANES)]
            group = (jnp.concatenate(rows, 1) >> 8) - part * (wide // 2)
            cols = pl.ds(pl.multiple_of(k * per, per), per)
            scatter_block(
                group, hot1[:, cols], high[:, cols], low[:, cols], left1, acc1, wide // 2
            )
            return 0

        lax.fori_loop(0, blocks * LANES // per, scatter, 0)
        for i in range(wide):
            moments[part * wide + i] = acc_row(acc1, i)
        inside = lax.rem(me, wide)

        def body(i, _):
            d = part * wide + lax.rem(inside + i, wide)
            copy_of(*back, me, d, d).start()
            return 0

        lax.fori_loop(last, wide, body, 0)

    own = lax.div(me, wide)

    def other(k, _):
        sum_slots(lax.rem(own + k, tiles // wide), 0)
        return 0

    lax.fori_loop(1, tiles // wide, other, 0)
    sum_slots(own, 1)
    returned[me] = moments[me]

    def wait_go(k, _):
        s = lax.rem(me + k, tiles)
        copy_of(*go, s, s, s).wait_recv()
        return 0

    lax.fori_loop(1, tiles, wait_go, 0)
    add_fields(received, slots, hot1, field_table, field_parts, new)

    acc2[...] = jnp.zeros(acc2.shape, F32)

    def collect(there, first):
        def body(i, _):
            s = there * PLANE + lax.rem(inner + i, PLANE)
            copy_of(*back, s, s, s).wait_recv()
            return 0

        lax.fori_loop(first, PLANE, body, 0)
        at = [there * PLANE + i for i in range(PLANE)]
        values = jnp.concatenate([returned[s] for s in at], 1)
        index = jnp.concatenate([lists[pl.ds(s, 1), :] for s in at], 1)
        top = values.astype(BF16)
        rest = (values - top.astype(F32)).astype(BF16)
        scatter_block(index >> 8, hot_rows(index), top, rest, left2, acc2, count // 2)

    collect(plane, 1)
    lax.fori_loop(
        1, planes, lambda k, _: (collect(lax.rem(plane + k, planes), 0), 0)[1], 0
    )
    for j in range(count):
        total = acc_row(acc2, j)
        weight = total[species : species + 1]
        mixed = scaled[j, 0:species, :] * weight
        mean = (total[:species] + mixed + fields[j, 0:species, :]) / (weight + 1.0)
        out[pl.ds(j, species, stride=count), :] = mean

    for i in range(4):

        @pl.when(sends[i])
        def _(i=i):
            halo_copy(i).wait_send()

    def finish(k, _):
        d = lax.rem(me + k, tiles)
        rate_copy(me, d, d).wait_send()
        copy_of(*go, me, d, d).wait_send()
        copy_of(*back, me, d, d).wait_send()
        return 0

    lax.fori_loop(1, tiles, finish, 0)


def hand_over(first, second, first_out, second_out, sems):
    copies = [
        pltpu.make_async_copy(first, first_out, sems.at[0]),
        pltpu.make_async_copy(second, second_out, sems.at[1]),
    ]
    for copy in copies:
        copy.start()
    for copy in copies:
        copy.wait()


def on_device(
    cell_means, diffusion, mix_rate, send_lists, compositions, weights, particle_slots, partners
):
    species, rows_x, rows_y, depth = cell_means.shape
    count = rows_x * rows_y
    tiles = send_lists.shape[1]
    particles = compositions.shape[1]
    blocks = particles // LANES
    vmem = lambda *shape: pltpu.VMEM(shape, F32)
    half_vmem = lambda *shape: pltpu.VMEM(shape, BF16)
    operands = (
        cell_means.reshape(species * count, depth),
        diffusion.reshape(count, depth),
        mix_rate.reshape(count, depth),
        send_lists[0],
        compositions,
        weights.reshape(blocks, LANES),
        particle_slots.reshape(blocks, LANES),
        partners.reshape(blocks, LANES),
    )
    out, new = pl.pallas_call(
        functools.partial(
            whole_kernel, lax.axis_size("gx"), lax.axis_size("gy"), rows_x, rows_y
        ),
        out_shape=(
            pltpu.VMEM((species * count, LANES), F32),
            pltpu.VMEM((species, particles), F32),
        ),
        in_specs=[pl.BlockSpec(memory_space=pltpu.HBM)] * 8,
        out_specs=[pl.BlockSpec(memory_space=pltpu.VMEM)] * 2,
        name="whole_kernel",
        scratch_shapes=[pltpu.VMEM(a.shape, a.dtype) for a in operands]
        + [
            vmem(rows_x, rows_y, ROWS, LANES),
            vmem(4, max(rows_x, rows_y), ROWS, LANES),
            vmem(count, ROWS, LANES),
            vmem(count, ROWS, LANES),
            vmem(tiles, 1, LANES),
            vmem(tiles, 1, LANES),
            vmem(blocks, LANES),
            vmem(tiles, ROWS, LANES),
            vmem(tiles, ROWS, LANES),
            vmem(tiles, ROWS, LANES),
            vmem(tiles, ROWS, LANES),
            half_vmem(particles // 256 * ROWS, 512),
            vmem(particles // 256 * ROWS, 256),
            vmem(ROWS, particles),
            half_vmem(ROWS, particles),
            half_vmem(ROWS, particles),
            half_vmem(256, particles),
            half_vmem(2 * PLANE * ROWS, 1024),
            vmem(2 * PLANE * ROWS, 256),
            half_vmem(tiles // 2 * ROWS, 512),
            vmem(tiles // 2 * ROWS, 256),
            half_vmem(count * ROWS, PLANE * LANES),
            vmem(count * ROWS, 256),
            pltpu.SemaphoreType.DMA((8,)),
            pltpu.SemaphoreType.DMA((4,)),
            pltpu.SemaphoreType.DMA((4,)),
            pltpu.SemaphoreType.DMA((tiles,)),
            pltpu.SemaphoreType.DMA((tiles,)),
            pltpu.SemaphoreType.DMA((tiles,)),
            pltpu.SemaphoreType.DMA((tiles,)),
            pltpu.SemaphoreType.DMA((tiles,)),
            pltpu.SemaphoreType.DMA((tiles,)),
        ],
        compiler_params=pltpu.CompilerParams(
            collective_id=0, has_side_effects=True, vmem_limit_bytes=63 * 1024 * 1024
        ),
    )(*operands)
    out, new = pl.pallas_call(
        hand_over,
        out_shape=tuple(jax.ShapeDtypeStruct(a.shape, a.dtype) for a in (out, new)),
        in_specs=[pl.BlockSpec(memory_space=pltpu.VMEM)] * 2,
        out_specs=[pl.BlockSpec(memory_space=pltpu.HBM)] * 2,
        scratch_shapes=[pltpu.SemaphoreType.DMA((2,))],
        compiler_params=pltpu.CompilerParams(vmem_limit_bytes=1024 * 1024),
        name="hand_over",
    )(out, new)
    return out.reshape(species, rows_x, rows_y, depth), new


def solution(mesh):
    in_specs = (
        P(None, "gx", "gy", None),
        P("gx", "gy", None),
        P("gx", "gy", None),
        P(("gx", "gy"), None, None),
        P(None, ("gx", "gy")),
        P(("gx", "gy")),
        P(("gx", "gy")),
        P(("gx", "gy")),
    )
    out_specs = (P(None, "gx", "gy", None), P(None, ("gx", "gy")))
    return jax.shard_map(
        on_device, mesh=mesh, in_specs=in_specs, out_specs=out_specs, check_vma=False
    )
```

```python
import functools

import jax
import jax.numpy as jnp
from jax import lax
from jax.experimental import pallas as pl
from jax.experimental.pallas import tpu as pltpu
from jax.sharding import PartitionSpec as P

PAIR_RATE = 0.3
LANES = 128
ROWS = 32
GROUPS = ROWS // 8
PLANE = 8
WIDE = 1024
FIRST = 0
HALO_ROUNDS = 2
F32 = jnp.float32
BF16 = jnp.bfloat16


def select_group(index, parts, groups):
    group = jnp.broadcast_to(index >> 8, (ROWS, index.shape[1]))
    total = jnp.zeros(group.shape, F32)
    for h in range(groups):
        total = jnp.where(group == h, parts[h * ROWS : (h + 1) * ROWS, :], total)
    return total


def row_block(table, k, width):
    many = width // LANES
    return jnp.concatenate([table[pl.ds(k * many + i, 1), :] for i in range(many)], 1)


def stencil(cells, halo, diffusion, fields, blend, scaled, table, rows_x, rows_y):
    lane = lax.broadcasted_iota(jnp.int32, (ROWS, LANES), 1)
    for x in range(rows_x):
        for y in range(rows_y):
            mid = cells[x, y]
            total = cells[x + 1, y] if x + 1 < rows_x else halo[1, y]
            total = total + (cells[x - 1, y] if x else halo[0, y])
            total = total + (cells[x, y + 1] if y + 1 < rows_y else halo[3, x])
            total = total + (cells[x, y - 1] if y else halo[2, x])
            total = total + jnp.where(lane < LANES - 1, pltpu.roll(mid, LANES - 1, 1), 0.0)
            total = total + jnp.where(lane > 0, pltpu.roll(mid, 1, 1), 0.0)
            j = x * rows_y + y
            filtered = mid + diffusion[j : j + 1, :] * (total - 6.0 * mid)
            fields[j] = filtered
            mixed = filtered * blend[j : j + 1, :]
            scaled[j] = mixed
            first = mixed.astype(BF16)
            rows = slice(j // 2 * ROWS, (j // 2 + 1) * ROWS)
            at = j % 2 * LANES
            table[rows, at : at + LANES] = first
            table[rows, 256 + at : 256 + at + LANES] = (mixed - first.astype(F32)).astype(BF16)


def scatter_block(group, hot, high, low, left, acc, groups):
    width = group.shape[1]
    group = jnp.broadcast_to(group.astype(F32).astype(BF16), (ROWS, width))
    for g in range(groups):
        mask = group == jnp.array(g, BF16)
        zero = jnp.zeros((ROWS, width), BF16)
        left[2 * g * ROWS : (2 * g + 1) * ROWS, :] = jnp.where(mask, high, zero)
        left[(2 * g + 1) * ROWS : (2 * g + 2) * ROWS, :] = jnp.where(mask, low, zero)
    acc[...] += lax.dot_general(
        left[...], hot, (((1,), (1,)), ((), ())), preferred_element_type=F32
    )


def hot_rows(index):
    place = lax.broadcasted_iota(jnp.int32, (256, index.shape[1]), 0)
    return jnp.where(place == (index & 255), 1.0, 0.0).astype(BF16)


def acc_row(acc, j):
    g, half = j // 2, (j % 2) * LANES
    return (
        acc[2 * g * ROWS : (2 * g + 1) * ROWS, half : half + LANES]
        + acc[(2 * g + 1) * ROWS : (2 * g + 2) * ROWS, half : half + LANES]
    )


def load_cells(means, cells, rows_x, rows_y):
    species = means.shape[0] // (rows_x * rows_y)
    for x in range(rows_x):
        for y in range(rows_y):
            j = x * rows_y + y
            cells[x, y, 0:species, :] = means[pl.ds(j, species, stride=rows_x * rows_y), :]
            cells[x, y, species:ROWS, :] = jnp.zeros((ROWS - species, LANES), F32)


def split_table(compositions, table):
    species, particles = compositions.shape
    for h in range(particles // 256):
        values = compositions[:, h * 256 : (h + 1) * 256]
        values = jnp.concatenate([values, jnp.zeros((ROWS - species, 256), F32)], 0)
        first = values.astype(BF16)
        table[h * ROWS : (h + 1) * ROWS, 0:256] = first
        table[h * ROWS : (h + 1) * ROWS, 256:512] = (values - first.astype(F32)).astype(BF16)


def gather_pairs(compositions, partners, table, parts, pair, first, last):
    species, particles = compositions.shape

    def body(k, _):
        index = row_block(partners, k, WIDE)
        hot = hot_rows(index)
        parts[...] = jnp.dot(
            table[...], jnp.concatenate([hot, hot], 0), preferred_element_type=F32
        )
        total = select_group(index, parts, particles // 256)
        at = pl.ds(pl.multiple_of(k * WIDE, WIDE), WIDE)
        pair[0:species, at] = PAIR_RATE * (compositions[:, at] - total[:species])
        return 0

    lax.fori_loop(first, last, body, 0)


def pick_rates(lists, rates, buffer):
    tiles = lists.shape[0]
    for first in range(0, tiles, 8):
        index = lists[first : first + 8, :]
        lane, chunk = index & (LANES - 1), index >> 7
        total = jnp.zeros((8, LANES), F32)
        for j in range(rates.shape[0]):
            row = jnp.broadcast_to(rates[j : j + 1, :], (8, LANES))
            found = jnp.take_along_axis(row, lane, axis=1, mode="promise_in_bounds")
            total = jnp.where(chunk == j, found, total)
        for i in range(8):
            buffer[first + i] = total[i : i + 1, :]


def spread_rates(slots, rates, out):
    blocks = slots.shape[0]
    parts = range(0, blocks, 8)
    lanes = [slots[b : b + 8, :] & (LANES - 1) for b in parts]
    chunks = [slots[b : b + 8, :] >> 7 for b in parts]

    def step(s, totals):
        row = jnp.broadcast_to(rates[s], (8, LANES))
        return tuple(
            jnp.where(
                chunk == s,
                jnp.take_along_axis(row, lane, axis=1, mode="promise_in_bounds"),
                total,
            )
            for lane, chunk, total in zip(lanes, chunks, totals)
        )

    start = tuple(jnp.zeros((8, LANES), F32) for _ in parts)
    totals = lax.fori_loop(0, rates.shape[0], step, start, unroll=8)
    for b, total in zip(parts, totals):
        out[b : b + 8, :] = total


def add_fields(received, slots, hot, table, parts, new):
    species, particles = new.shape
    groups = table.shape[0] // ROWS

    def chunk(c, _):
        for h in range(groups):
            s = 2 * (c * groups + h)
            values = jnp.concatenate([received[s], received[s + 1]], 1)
            first = values.astype(BF16)
            rows = slice(h * ROWS, (h + 1) * ROWS)
            table[rows, 0:256] = first
            table[rows, 256:512] = (values - first.astype(F32)).astype(BF16)

        def body(k, _):
            at = pl.ds(pl.multiple_of(k * WIDE, WIDE), WIDE)
            both = hot[:, at]
            parts[...] = jnp.dot(
                table[...], jnp.concatenate([both, both], 0), preferred_element_type=F32
            )
            index = row_block(slots, k, WIDE) - c * (groups * 256)
            new[:, at] += select_group(index, parts, groups)[:species]
            return 0

        return lax.fori_loop(0, particles // WIDE, body, 0)

    lax.fori_loop(0, received.shape[0] // 2 // groups, chunk, 0)


def whole_kernel(
    nx, ny, rows_x, rows_y, *refs
):
    inputs, (out, new), refs = refs[:8], refs[8:10], refs[10:]
    staged, refs = refs[:8], refs[8:]
    means, diffusion, rate, lists, compositions, weights, slots, partners = staged
    (
        cells, halo, fields, scaled, rates_out, rates_in, rates, outgoing, received, moments,
        returned, table, parts, pair, high, low, hot1, hot2, left1, acc1, field_table, left2, acc2,
        in_sems, halo_send, halo_recv, rate_send, rate_recv, go_send, go_recv,
        back_send, back_recv, late,
    ) = refs
    tiles = nx * ny
    planes = tiles // PLANE
    count = rows_x * rows_y
    species = compositions.shape[0]
    blocks = slots.shape[0]
    gx, gy = lax.axis_index("gx"), lax.axis_index("gy")
    me = gx * ny + gy
    plane, inner = lax.div(me, PLANE), lax.rem(me, PLANE)

    def place(d):
        return (lax.div(d, ny), lax.rem(d, ny))

    loads = [
        pltpu.make_async_copy(inputs[i], staged[i], in_sems.at[i]) for i in range(8)
    ]
    for i in (0, 4, 7, 2, 3, 6, 1, 5):
        loads[i].start()

    barrier = pltpu.get_barrier_semaphore()

    def signal(semaphore, d):
        pl.semaphore_signal(
            semaphore, inc=1, device_id=place(d), device_id_type=pl.DeviceIdType.MESH
        )

    def greet_plane(k, _):
        signal(barrier, plane * PLANE + lax.rem(inner + k, PLANE))
        return 0

    def greet(d, _):
        signal(barrier, d)
        return 0

    def announce(d, _):
        signal(late, d)
        return 0

    lax.fori_loop(1, PLANE, greet_plane, 0)
    above = jnp.logical_and(gx < nx - 1, lax.div(me + ny, PLANE) > plane)
    below = jnp.logical_and(gx > 0, lax.div(me - ny + tiles, PLANE) < plane + planes)

    @pl.when(below)
    def _():
        signal(barrier, me - ny)

    lax.fori_loop((plane + 1) * PLANE, tiles, greet, 0)

    loads[0].wait()
    for x in range(rows_x):
        for y in range(rows_y):
            j = x * rows_y + y
            cells[x, y, 0:species, :] = means[pl.ds(j, species, stride=count), :]
            cells[x, y, species:ROWS, :] = jnp.zeros((ROWS - species, LANES), F32)

    rounds = blocks * LANES // WIDE
    hops = lax.div(gx, 2) + lax.rem(gx, 2) + lax.div(gy, 2)
    early = jnp.where(hops == 0, FIRST, 0)
    early = jnp.minimum(early, rounds)
    soon = jnp.minimum(early + HALO_ROUNDS, rounds)
    loads[4].wait()
    loads[7].wait()
    split_table(compositions, table)
    gather_pairs(compositions, partners, table, parts, pair, 0, early)

    pl.semaphore_wait(barrier, (plane + 1) * PLANE - 1 + above.astype(jnp.int32))

    def halo_copy(i):
        source, length, target = (
            (cells.at[rows_x - 1, :, 0:species], rows_y, (gx + 1, gy)),
            (cells.at[0, :, 0:species], rows_y, (gx - 1, gy)),
            (cells.at[:, rows_y - 1, 0:species], rows_x, (gx, gy + 1)),
            (cells.at[:, 0, 0:species], rows_x, (gx, gy - 1)),
        )[i]
        return pltpu.make_async_remote_copy(
            src_ref=source,
            dst_ref=halo.at[i, 0:length, 0:species],
            send_sem=halo_send.at[i],
            recv_sem=halo_recv.at[i],
            device_id=target,
            device_id_type=pl.DeviceIdType.MESH,
        )

    sends = (gx < nx - 1, gx > 0, gy < ny - 1, gy > 0)
    receives = (gx > 0, gx < nx - 1, gy > 0, gy < ny - 1)
    for i in range(4):

        @pl.when(sends[i])
        def _(i=i):
            halo_copy(i).start()

    lax.fori_loop(0, plane * PLANE, announce, 0)
    for i in range(4):
        halo[i, :, species:ROWS] = jnp.zeros(halo[i, :, species:ROWS].shape, F32)

        @pl.when(jnp.logical_not(receives[i]))
        def _(i=i):
            halo[i, :, 0:species] = jnp.zeros(halo[i, :, 0:species].shape, F32)

    loads[2].wait()
    loads[3].wait()
    blend = 1.0 - jnp.exp(-rate[...])
    pick_rates(lists, blend, rates_out)
    rates_in[me] = rates_out[me]

    def rate_copy(source, d, target):
        return pltpu.make_async_remote_copy(
            src_ref=rates_out.at[d],
            dst_ref=rates_in.at[source],
            send_sem=rate_send.at[d],
            recv_sem=rate_recv.at[source],
            device_id=place(target),
            device_id_type=pl.DeviceIdType.MESH,
        )

    def send_rates(k, _):
        d = lax.rem(me + k, tiles)
        rate_copy(me, d, d).start()
        return 0


    loads[6].wait()
    for b in range(0, blocks, 4):
        hot1[:, b * LANES : (b + 4) * LANES] = hot_rows(row_block(slots, b // 4, 4 * LANES))
    for b in range(0, tiles, 4):
        hot2[:, b * LANES : (b + 4) * LANES] = hot_rows(row_block(lists, b // 4, 4 * LANES))
    loads[1].wait()
    gather_pairs(compositions, partners, table, parts, pair, early, soon)

    @pl.when(plane < planes - 1)
    def _():
        pl.semaphore_wait(late, tiles - (plane + 1) * PLANE)

    lax.fori_loop(1, tiles, send_rates, 0)

    def go_copy(source, d, target):
        return pltpu.make_async_remote_copy(
            src_ref=outgoing.at[d, 0:species],
            dst_ref=received.at[source, 0:species],
            send_sem=go_send.at[d],
            recv_sem=go_recv.at[source],
            device_id=place(target),
            device_id_type=pl.DeviceIdType.MESH,
        )

    def back_copy(source, d, target):
        return pltpu.make_async_remote_copy(
            src_ref=moments.at[d, 0 : species + 1],
            dst_ref=returned.at[source, 0 : species + 1],
            send_sem=back_send.at[d],
            recv_sem=back_recv.at[source],
            device_id=place(target),
            device_id_type=pl.DeviceIdType.MESH,
        )

    wide = acc1.shape[0] // ROWS
    sections = tiles // wide
    own = lax.div(me, wide)
    per_section = wide // PLANE

    def peer(section, k):
        turn = lax.div(k, PLANE)
        near = lax.rem(plane + 1 + turn, per_section)
        turn = jnp.where(section == own, near, turn)
        return section * wide + turn * PLANE + lax.rem(inner + k, PLANE)

    def fill(there):
        at = pl.ds(pl.multiple_of(there * (PLANE * LANES), PLANE * LANES), PLANE * LANES)
        hot = hot2[:, at]
        parts[0 : count // 2 * ROWS, :] = jnp.dot(
            field_table[...], jnp.concatenate([hot, hot], 0), preferred_element_type=F32
        )
        index = row_block(lists, there, PLANE * LANES)
        found = select_group(index, parts, count // 2)
        for i in range(PLANE):
            outgoing[there * PLANE + i] = found[:, i * LANES : (i + 1) * LANES]

    def send_go(there, first):
        def body(k, _):
            d = there * PLANE + lax.rem(inner + k, PLANE)
            go_copy(me, d, d).start()
            return 0

        lax.fori_loop(first, PLANE, body, 0)

    def far_plane(k):
        return lax.rem(own * per_section + k, planes)

    for i in range(4):

        @pl.when(receives[i])
        def _(i=i):
            halo_copy(i).wait_recv()

    stencil(
        cells, halo, diffusion, fields, blend, scaled, field_table, rows_x, rows_y
    )

    def go_far(k, _):
        fill(far_plane(k))
        send_go(far_plane(k), 0)
        return 0

    lax.fori_loop(per_section, planes, go_far, 0)
    gather_pairs(compositions, partners, table, parts, pair, soon, rounds)
    loads[5].wait()

    def wait_rates(k, _):
        s = lax.rem(me + k, tiles)
        rate_copy(s, s, s).wait_recv()
        return 0

    lax.fori_loop(1, tiles, wait_rates, 0)
    spread_rates(slots, rates_in, rates)

    def weigh(b, _):
        at = pl.ds(pl.multiple_of(b * LANES, LANES), LANES)
        mine = compositions[:, at]
        fresh = mine - rates[pl.ds(b, 1), :] * mine - pair[0:species, at]
        new[:, at] = fresh
        weight = weights[pl.ds(b, 1), :]
        values = jnp.concatenate(
            [weight * fresh, weight, jnp.zeros((ROWS - species - 1, LANES), F32)], 0
        )
        top = values.astype(BF16)
        high[:, at] = top
        low[:, at] = (values - top.astype(F32)).astype(BF16)
        return 0

    lax.fori_loop(0, blocks, weigh, 0, unroll=4)

    per = left1.shape[1]

    def sum_slots(section):
        acc1[...] = jnp.zeros(acc1.shape, F32)

        def scatter(k, _):
            group = (row_block(slots, k, per) >> 8) - section * (wide // 2)
            cols = pl.ds(pl.multiple_of(k * per, per), per)
            scatter_block(
                group, hot1[:, cols], high[:, cols], low[:, cols], left1, acc1, wide // 2
            )
            return 0

        lax.fori_loop(0, blocks * LANES // per, scatter, 0)
        for i in range(wide):
            moments[section * wide + i] = acc_row(acc1, i)

    def send_back(section, first, last):
        def body(k, _):
            d = peer(section, k)
            back_copy(me, d, d).start()
            return 0

        lax.fori_loop(first, last, body, 0)

    def other(r, _):
        section = lax.rem(own + r, sections)
        sum_slots(section)
        send_back(section, 0, wide)
        return 0

    lax.fori_loop(1, sections, other, 0)

    def go_near(k, _):
        there = own * per_section + lax.rem(plane + k, per_section)
        fill(there)
        send_go(there, 0)
        return 0

    lax.fori_loop(1, per_section, go_near, 0)
    fill(plane)
    received[me] = outgoing[me]
    send_go(plane, 1)
    sum_slots(own)
    send_back(own, 0, wide - PLANE)
    send_back(own, wide - PLANE + 1, wide)
    returned[me] = moments[me]

    def wait_go(k, _):
        s = lax.rem(me + k, tiles)
        go_copy(s, s, s).wait_recv()
        return 0

    lax.fori_loop(1, tiles, wait_go, 0)
    add_fields(received, slots, hot1, table, parts, new)

    for i in range(4):

        @pl.when(sends[i])
        def _(i=i):
            halo_copy(i).wait_send()

    def sent(k, _):
        d = lax.rem(me + k, tiles)
        rate_copy(me, d, d).wait_send()
        go_copy(me, d, d).wait_send()
        return 0

    lax.fori_loop(1, tiles, sent, 0)

    acc2[...] = jnp.zeros(acc2.shape, F32)

    def collect(there, first):
        def body(i, _):
            s = there * PLANE + lax.rem(inner + i, PLANE)
            back_copy(s, s, s).wait_recv()
            return 0

        lax.fori_loop(first, PLANE, body, 0)
        at = [there * PLANE + i for i in range(PLANE)]
        values = jnp.concatenate([returned[s] for s in at], 1)
        index = jnp.concatenate([lists[pl.ds(s, 1), :] for s in at], 1)
        top = values.astype(BF16)
        rest = (values - top.astype(F32)).astype(BF16)
        cols = pl.ds(pl.multiple_of(there * (PLANE * LANES), PLANE * LANES), PLANE * LANES)
        scatter_block(index >> 8, hot2[:, cols], top, rest, left2, acc2, count // 2)

    collect(plane, 1)
    near = own * per_section

    def collect_near(k, _):
        collect(near + lax.rem(plane + k, per_section), 0)
        return 0

    lax.fori_loop(1, per_section, collect_near, 0)

    def collect_far(k, _):
        collect(far_plane(k), 0)
        return 0

    lax.fori_loop(per_section, planes - 1, collect_far, 0)

    def finish(k, _):
        d = lax.rem(me + k, tiles)
        back_copy(me, d, d).wait_send()
        return 0

    lax.fori_loop(1, tiles, finish, 0)
    collect(far_plane(planes - 1), 0)
    for j in range(count):
        total = acc_row(acc2, j)
        weight = total[species : species + 1]
        mixed = scaled[j, 0:species, :] * weight
        mean = total[:species] + mixed + fields[j, 0:species, :]
        out[pl.ds(j, species, stride=count), :] = mean * (1.0 / (weight + 1.0))


def hand_over(first, second, first_out, second_out, sems):
    copies = [
        pltpu.make_async_copy(first, first_out, sems.at[0]),
        pltpu.make_async_copy(second, second_out, sems.at[1]),
    ]
    for copy in copies:
        copy.start()
    for copy in copies:
        copy.wait()


def on_device(
    cell_means, diffusion, mix_rate, send_lists, compositions, weights, particle_slots, partners
):
    species, rows_x, rows_y, depth = cell_means.shape
    count = rows_x * rows_y
    tiles = send_lists.shape[1]
    particles = compositions.shape[1]
    blocks = particles // LANES
    vmem = lambda *shape: pltpu.VMEM(shape, F32)
    half_vmem = lambda *shape: pltpu.VMEM(shape, BF16)
    operands = (
        cell_means.reshape(species * count, depth),
        diffusion.reshape(count, depth),
        mix_rate.reshape(count, depth),
        send_lists[0],
        compositions,
        weights.reshape(blocks, LANES),
        particle_slots.reshape(blocks, LANES),
        partners.reshape(blocks, LANES),
    )
    out, new = pl.pallas_call(
        functools.partial(
            whole_kernel, lax.axis_size("gx"), lax.axis_size("gy"), rows_x, rows_y
        ),
        out_shape=(
            pltpu.VMEM((species * count, LANES), F32),
            pltpu.VMEM((species, particles), F32),
        ),
        in_specs=[pl.BlockSpec(memory_space=pltpu.HBM)] * 8,
        out_specs=[pl.BlockSpec(memory_space=pltpu.VMEM)] * 2,
        name="whole_kernel",
        scratch_shapes=[pltpu.VMEM(a.shape, a.dtype) for a in operands]
        + [
            vmem(rows_x, rows_y, ROWS, LANES),
            vmem(4, max(rows_x, rows_y), ROWS, LANES),
            vmem(count, ROWS, LANES),
            vmem(count, ROWS, LANES),
            vmem(tiles, 1, LANES),
            vmem(tiles, 1, LANES),
            vmem(blocks, LANES),
            vmem(tiles, ROWS, LANES),
            vmem(tiles, ROWS, LANES),
            vmem(tiles, ROWS, LANES),
            vmem(tiles, ROWS, LANES),
            half_vmem(particles // 256 * ROWS, 512),
            vmem(particles // 256 * ROWS, WIDE),
            vmem(ROWS, particles),
            half_vmem(ROWS, particles),
            half_vmem(ROWS, particles),
            half_vmem(256, particles),
            half_vmem(256, tiles * LANES),
            half_vmem(2 * PLANE * ROWS, 1024),
            vmem(2 * PLANE * ROWS, 256),
            half_vmem(count // 2 * ROWS, 512),
            half_vmem(count * ROWS, PLANE * LANES),
            vmem(count * ROWS, 256),
            pltpu.SemaphoreType.DMA((8,)),
            pltpu.SemaphoreType.DMA((4,)),
            pltpu.SemaphoreType.DMA((4,)),
            pltpu.SemaphoreType.DMA((tiles,)),
            pltpu.SemaphoreType.DMA((tiles,)),
            pltpu.SemaphoreType.DMA((tiles,)),
            pltpu.SemaphoreType.DMA((tiles,)),
            pltpu.SemaphoreType.DMA((tiles,)),
            pltpu.SemaphoreType.DMA((tiles,)),
            pltpu.SemaphoreType.REGULAR,
        ],
        compiler_params=pltpu.CompilerParams(
            collective_id=0, has_side_effects=True, vmem_limit_bytes=63 * 1024 * 1024
        ),
    )(*operands)
    out, new = pl.pallas_call(
        hand_over,
        out_shape=tuple(jax.ShapeDtypeStruct(a.shape, a.dtype) for a in (out, new)),
        in_specs=[pl.BlockSpec(memory_space=pltpu.VMEM)] * 2,
        out_specs=[pl.BlockSpec(memory_space=pltpu.HBM)] * 2,
        scratch_shapes=[pltpu.SemaphoreType.DMA((2,))],
        compiler_params=pltpu.CompilerParams(vmem_limit_bytes=1024 * 1024),
        name="hand_over",
    )(out, new)
    return out.reshape(species, rows_x, rows_y, depth), new


def solution(mesh):
    in_specs = (
        P(None, "gx", "gy", None),
        P("gx", "gy", None),
        P("gx", "gy", None),
        P(("gx", "gy"), None, None),
        P(None, ("gx", "gy")),
        P(("gx", "gy")),
        P(("gx", "gy")),
        P(("gx", "gy")),
    )
    out_specs = (P(None, "gx", "gy", None), P(None, ("gx", "gy")))
    return jax.shard_map(
        on_device, mesh=mesh, in_specs=in_specs, out_specs=out_specs, check_vma=False
    )
```

```python
import functools

import jax
import jax.numpy as jnp
from jax import lax
from jax.experimental import pallas as pl
from jax.experimental.pallas import tpu as pltpu
from jax.sharding import PartitionSpec as P

PAIR_RATE = 0.3
LANES = 128
ROWS = 32
GROUPS = ROWS // 8
PLANE = 8
WIDE = 1024
FIRST = 0
LAST = 4
HALO_ROUNDS = 2
F32 = jnp.float32
BF16 = jnp.bfloat16


def select_group(index, parts, groups):
    group = jnp.broadcast_to(index >> 8, (ROWS, index.shape[1]))
    total = jnp.zeros(group.shape, F32)
    for h in range(groups):
        total = jnp.where(group == h, parts[h * ROWS : (h + 1) * ROWS, :], total)
    return total


def row_block(table, k, width):
    many = width // LANES
    return jnp.concatenate([table[pl.ds(k * many + i, 1), :] for i in range(many)], 1)


def stencil(cells, halo, diffusion, fields, blend, scaled, table, rows_x, rows_y):
    lane = lax.broadcasted_iota(jnp.int32, (ROWS, LANES), 1)
    for x in range(rows_x):
        for y in range(rows_y):
            mid = cells[x, y]
            total = cells[x + 1, y] if x + 1 < rows_x else halo[1, y]
            total = total + (cells[x - 1, y] if x else halo[0, y])
            total = total + (cells[x, y + 1] if y + 1 < rows_y else halo[3, x])
            total = total + (cells[x, y - 1] if y else halo[2, x])
            total = total + jnp.where(lane < LANES - 1, pltpu.roll(mid, LANES - 1, 1), 0.0)
            total = total + jnp.where(lane > 0, pltpu.roll(mid, 1, 1), 0.0)
            j = x * rows_y + y
            filtered = mid + diffusion[j : j + 1, :] * (total - 6.0 * mid)
            fields[j] = filtered
            mixed = filtered * blend[j : j + 1, :]
            scaled[j] = mixed
            first = mixed.astype(BF16)
            rows = slice(j // 2 * ROWS, (j // 2 + 1) * ROWS)
            at = j % 2 * LANES
            table[rows, at : at + LANES] = first
            table[rows, 256 + at : 256 + at + LANES] = (mixed - first.astype(F32)).astype(BF16)


def scatter_block(group, hot, high, low, left, acc, groups):
    width = group.shape[1]
    group = jnp.broadcast_to(group.astype(F32).astype(BF16), (ROWS, width))
    for g in range(groups):
        mask = group == jnp.array(g, BF16)
        zero = jnp.zeros((ROWS, width), BF16)
        left[2 * g * ROWS : (2 * g + 1) * ROWS, :] = jnp.where(mask, high, zero)
        left[(2 * g + 1) * ROWS : (2 * g + 2) * ROWS, :] = jnp.where(mask, low, zero)
    acc[...] += lax.dot_general(
        left[...], hot, (((1,), (1,)), ((), ())), preferred_element_type=F32
    )


def hot_rows(index):
    place = lax.broadcasted_iota(jnp.int32, (256, index.shape[1]), 0)
    return jnp.where(place == (index & 255), 1.0, 0.0).astype(BF16)


def acc_row(acc, j):
    g, half = j // 2, (j % 2) * LANES
    return (
        acc[2 * g * ROWS : (2 * g + 1) * ROWS, half : half + LANES]
        + acc[(2 * g + 1) * ROWS : (2 * g + 2) * ROWS, half : half + LANES]
    )


def load_cells(means, cells, rows_x, rows_y):
    species = means.shape[0] // (rows_x * rows_y)
    for x in range(rows_x):
        for y in range(rows_y):
            j = x * rows_y + y
            cells[x, y, 0:species, :] = means[pl.ds(j, species, stride=rows_x * rows_y), :]
            cells[x, y, species:ROWS, :] = jnp.zeros((ROWS - species, LANES), F32)


def split_table(compositions, table):
    species, particles = compositions.shape
    for h in range(particles // 256):
        values = compositions[:, h * 256 : (h + 1) * 256]
        values = jnp.concatenate([values, jnp.zeros((ROWS - species, 256), F32)], 0)
        first = values.astype(BF16)
        table[h * ROWS : (h + 1) * ROWS, 0:256] = first
        table[h * ROWS : (h + 1) * ROWS, 256:512] = (values - first.astype(F32)).astype(BF16)


def gather_pairs(compositions, partners, table, parts, pair, first, last):
    species, particles = compositions.shape

    def body(k, _):
        index = row_block(partners, k, WIDE)
        hot = hot_rows(index)
        parts[...] = jnp.dot(
            table[...], jnp.concatenate([hot, hot], 0), preferred_element_type=F32
        )
        total = select_group(index, parts, particles // 256)
        at = pl.ds(pl.multiple_of(k * WIDE, WIDE), WIDE)
        pair[0:species, at] = PAIR_RATE * (compositions[:, at] - total[:species])
        return 0

    lax.fori_loop(first, last, body, 0)


def pick_rates(lists, rates, buffer):
    tiles = lists.shape[0]
    for first in range(0, tiles, 8):
        index = lists[first : first + 8, :]
        lane, chunk = index & (LANES - 1), index >> 7
        total = jnp.zeros((8, LANES), F32)
        for j in range(rates.shape[0]):
            row = jnp.broadcast_to(rates[j : j + 1, :], (8, LANES))
            found = jnp.take_along_axis(row, lane, axis=1, mode="promise_in_bounds")
            total = jnp.where(chunk == j, found, total)
        for i in range(8):
            buffer[first + i] = total[i : i + 1, :]


def spread_rates(slots, rates, out):
    blocks = slots.shape[0]
    parts = range(0, blocks, 8)
    lanes = [slots[b : b + 8, :] & (LANES - 1) for b in parts]
    chunks = [slots[b : b + 8, :] >> 7 for b in parts]

    def step(s, totals):
        row = jnp.broadcast_to(rates[s], (8, LANES))
        return tuple(
            jnp.where(
                chunk == s,
                jnp.take_along_axis(row, lane, axis=1, mode="promise_in_bounds"),
                total,
            )
            for lane, chunk, total in zip(lanes, chunks, totals)
        )

    start = tuple(jnp.zeros((8, LANES), F32) for _ in parts)
    totals = lax.fori_loop(0, rates.shape[0], step, start, unroll=8)
    for b, total in zip(parts, totals):
        out[b : b + 8, :] = total


def add_fields(received, slots, hot, table, parts, new, section, groups):
    species, particles = new.shape
    for h in range(groups):
        s = 2 * (section * groups + h)
        values = jnp.concatenate([received[s], received[s + 1]], 1)
        first = values.astype(BF16)
        rows = slice(h * ROWS, (h + 1) * ROWS)
        table[rows, 0:256] = first
        table[rows, 256:512] = (values - first.astype(F32)).astype(BF16)

    def body(k, _):
        at = pl.ds(pl.multiple_of(k * WIDE, WIDE), WIDE)
        both = hot[:, at]
        parts[0 : groups * ROWS, :] = jnp.dot(
            table[0 : groups * ROWS, :],
            jnp.concatenate([both, both], 0),
            preferred_element_type=F32,
        )
        index = row_block(slots, k, WIDE) - section * (groups * 256)
        new[:, at] += select_group(index, parts, groups)[:species]
        return 0

    lax.fori_loop(0, particles // WIDE, body, 0)


def whole_kernel(
    nx, ny, rows_x, rows_y, *refs
):
    inputs, (out, new), refs = refs[:8], refs[8:10], refs[10:]
    staged, refs = refs[:8], refs[8:]
    means, diffusion, rate, lists, compositions, weights, slots, partners = staged
    (
        cells, halo, fields, scaled, rates_out, rates_in, rates, outgoing, received, moments,
        returned, table, parts, pair, high, low, hot1, hot2, left1, acc1, field_table, left2, acc2,
        in_sems, halo_send, halo_recv, rate_send, rate_recv, go_send, go_recv,
        back_send, back_recv, late,
    ) = refs
    tiles = nx * ny
    planes = tiles // PLANE
    count = rows_x * rows_y
    species = compositions.shape[0]
    blocks = slots.shape[0]
    gx, gy = lax.axis_index("gx"), lax.axis_index("gy")
    me = gx * ny + gy
    plane, inner = lax.div(me, PLANE), lax.rem(me, PLANE)

    def place(d):
        return (lax.div(d, ny), lax.rem(d, ny))

    loads = [
        pltpu.make_async_copy(inputs[i], staged[i], in_sems.at[i]) for i in range(8)
    ]
    for i in (0, 4, 7, 2, 3, 6, 1, 5):
        loads[i].start()

    barrier = pltpu.get_barrier_semaphore()

    def signal(semaphore, d):
        pl.semaphore_signal(
            semaphore, inc=1, device_id=place(d), device_id_type=pl.DeviceIdType.MESH
        )

    def greet_plane(k, _):
        signal(barrier, plane * PLANE + lax.rem(inner + k, PLANE))
        return 0

    def greet(d, _):
        signal(barrier, d)
        return 0

    def announce(d, _):
        signal(late, d)
        return 0

    lax.fori_loop(1, PLANE, greet_plane, 0)
    above = jnp.logical_and(gx < nx - 1, lax.div(me + ny, PLANE) > plane)
    below = jnp.logical_and(gx > 0, lax.div(me - ny + tiles, PLANE) < plane + planes)

    @pl.when(below)
    def _():
        signal(barrier, me - ny)

    lax.fori_loop((plane + 1) * PLANE, tiles, greet, 0)

    loads[0].wait()
    for x in range(rows_x):
        for y in range(rows_y):
            j = x * rows_y + y
            cells[x, y, 0:species, :] = means[pl.ds(j, species, stride=count), :]
            cells[x, y, species:ROWS, :] = jnp.zeros((ROWS - species, LANES), F32)

    pl.semaphore_wait(barrier, (plane + 1) * PLANE - 1 + above.astype(jnp.int32))

    def halo_copy(i):
        source, length, target = (
            (cells.at[rows_x - 1, :, 0:species], rows_y, (gx + 1, gy)),
            (cells.at[0, :, 0:species], rows_y, (gx - 1, gy)),
            (cells.at[:, rows_y - 1, 0:species], rows_x, (gx, gy + 1)),
            (cells.at[:, 0, 0:species], rows_x, (gx, gy - 1)),
        )[i]
        return pltpu.make_async_remote_copy(
            src_ref=source,
            dst_ref=halo.at[i, 0:length, 0:species],
            send_sem=halo_send.at[i],
            recv_sem=halo_recv.at[i],
            device_id=target,
            device_id_type=pl.DeviceIdType.MESH,
        )

    sends = (gx < nx - 1, gx > 0, gy < ny - 1, gy > 0)
    receives = (gx > 0, gx < nx - 1, gy > 0, gy < ny - 1)
    for i in (2, 3, 0, 1):

        @pl.when(sends[i])
        def _(i=i):
            halo_copy(i).start()

    lax.fori_loop(0, plane * PLANE, announce, 0)
    for i in range(4):
        halo[i, :, species:ROWS] = jnp.zeros(halo[i, :, species:ROWS].shape, F32)

        @pl.when(jnp.logical_not(receives[i]))
        def _(i=i):
            halo[i, :, 0:species] = jnp.zeros(halo[i, :, 0:species].shape, F32)

    rounds = blocks * LANES // WIDE
    hops = lax.div(gx, 2) + lax.rem(gx, 2) + lax.div(gy, 2)
    early = jnp.where(hops == 0, FIRST, 0)
    early = jnp.minimum(early, rounds)
    soon = jnp.minimum(early + HALO_ROUNDS, rounds)
    loads[4].wait()
    loads[7].wait()
    split_table(compositions, table)
    gather_pairs(compositions, partners, table, parts, pair, 0, early)

    loads[2].wait()
    loads[3].wait()
    blend = 1.0 - jnp.exp(-rate[...])
    pick_rates(lists, blend, rates_out)
    rates_in[me] = rates_out[me]

    def rate_copy(source, d, target):
        return pltpu.make_async_remote_copy(
            src_ref=rates_out.at[d],
            dst_ref=rates_in.at[source],
            send_sem=rate_send.at[d],
            recv_sem=rate_recv.at[source],
            device_id=place(target),
            device_id_type=pl.DeviceIdType.MESH,
        )

    def send_rates(k, _):
        d = lax.rem(me + k, tiles)
        rate_copy(me, d, d).start()
        return 0


    loads[6].wait()
    for b in range(0, blocks, 4):
        hot1[:, b * LANES : (b + 4) * LANES] = hot_rows(row_block(slots, b // 4, 4 * LANES))
    for b in range(0, tiles, 4):
        hot2[:, b * LANES : (b + 4) * LANES] = hot_rows(row_block(lists, b // 4, 4 * LANES))
    loads[1].wait()
    gather_pairs(compositions, partners, table, parts, pair, early, soon)

    @pl.when(plane < planes - 1)
    def _():
        pl.semaphore_wait(late, tiles - (plane + 1) * PLANE)

    lax.fori_loop(1, tiles, send_rates, 0)

    def go_copy(source, d, target):
        return pltpu.make_async_remote_copy(
            src_ref=outgoing.at[d, 0:species],
            dst_ref=received.at[source, 0:species],
            send_sem=go_send.at[d],
            recv_sem=go_recv.at[source],
            device_id=place(target),
            device_id_type=pl.DeviceIdType.MESH,
        )

    def back_copy(source, d, target):
        return pltpu.make_async_remote_copy(
            src_ref=moments.at[d, 0 : species + 1],
            dst_ref=returned.at[source, 0 : species + 1],
            send_sem=back_send.at[d],
            recv_sem=back_recv.at[source],
            device_id=place(target),
            device_id_type=pl.DeviceIdType.MESH,
        )

    wide = acc1.shape[0] // ROWS
    sections = tiles // wide
    own = lax.div(me, wide)
    per_section = wide // PLANE

    def peer(section, k):
        turn = lax.div(k, PLANE)
        near = lax.rem(plane + 1 + turn, per_section)
        turn = jnp.where(section == own, near, turn)
        return section * wide + turn * PLANE + lax.rem(inner + k, PLANE)

    def fill(there):
        at = pl.ds(pl.multiple_of(there * (PLANE * LANES), PLANE * LANES), PLANE * LANES)
        hot = hot2[:, at]
        parts[0 : count // 2 * ROWS, :] = jnp.dot(
            field_table[...], jnp.concatenate([hot, hot], 0), preferred_element_type=F32
        )
        index = row_block(lists, there, PLANE * LANES)
        found = select_group(index, parts, count // 2)
        for i in range(PLANE):
            outgoing[there * PLANE + i] = found[:, i * LANES : (i + 1) * LANES]

    def send_go(there, first):
        def body(k, _):
            d = there * PLANE + lax.rem(inner + k, PLANE)
            go_copy(me, d, d).start()
            return 0

        lax.fori_loop(first, PLANE, body, 0)

    def far_plane(k):
        return lax.rem(own * per_section + k, planes)

    for i in range(4):

        @pl.when(receives[i])
        def _(i=i):
            halo_copy(i).wait_recv()

    stencil(
        cells, halo, diffusion, fields, blend, scaled, field_table, rows_x, rows_y
    )

    def go_far(k, _):
        fill(far_plane(k))
        send_go(far_plane(k), 0)
        return 0

    lax.fori_loop(per_section, planes, go_far, 0)
    gather_pairs(compositions, partners, table, parts, pair, soon, rounds)
    loads[5].wait()

    def wait_rates(k, _):
        s = lax.rem(me + k, tiles)
        rate_copy(s, s, s).wait_recv()
        return 0

    lax.fori_loop(1, tiles, wait_rates, 0)
    spread_rates(slots, rates_in, rates)

    def weigh(b, _):
        at = pl.ds(pl.multiple_of(b * LANES, LANES), LANES)
        mine = compositions[:, at]
        fresh = mine - rates[pl.ds(b, 1), :] * mine - pair[0:species, at]
        new[:, at] = fresh
        weight = weights[pl.ds(b, 1), :]
        values = jnp.concatenate(
            [weight * fresh, weight, jnp.zeros((ROWS - species - 1, LANES), F32)], 0
        )
        top = values.astype(BF16)
        high[:, at] = top
        low[:, at] = (values - top.astype(F32)).astype(BF16)
        return 0

    lax.fori_loop(0, blocks, weigh, 0, unroll=4)

    per = left1.shape[1]

    def sum_slots(section):
        acc1[...] = jnp.zeros(acc1.shape, F32)

        def scatter(k, _):
            group = (row_block(slots, k, per) >> 8) - section * (wide // 2)
            cols = pl.ds(pl.multiple_of(k * per, per), per)
            scatter_block(
                group, hot1[:, cols], high[:, cols], low[:, cols], left1, acc1, wide // 2
            )
            return 0

        lax.fori_loop(0, blocks * LANES // per, scatter, 0)
        for i in range(wide):
            moments[section * wide + i] = acc_row(acc1, i)

    def send_back(section, first, last):
        def body(k, _):
            d = peer(section, k)
            back_copy(me, d, d).start()
            return 0

        lax.fori_loop(first, last, body, 0)

    def other(r, _):
        section = lax.rem(own + r, sections)
        sum_slots(section)
        send_back(section, 0, wide)
        return 0

    lax.fori_loop(1, sections, other, 0)

    def go_near(k, _):
        there = own * per_section + lax.rem(plane + k, per_section)
        fill(there)
        send_go(there, 0)
        return 0

    lax.fori_loop(1, per_section, go_near, 0)
    fill(plane)
    received[me] = outgoing[me]
    send_go(plane, 1)
    sum_slots(own)
    send_back(own, 0, wide - PLANE)
    send_back(own, wide - PLANE + 1, wide)
    returned[me] = moments[me]

    def wait_go(s, _):
        go_copy(s, s, s).wait_recv()
        return 0

    def add_section(section):
        add_fields(received, slots, hot1, table, parts, new, section, wide // 2)

    lax.fori_loop(own * wide, me, wait_go, 0)
    lax.fori_loop(me + 1, (own + 1) * wide, wait_go, 0)
    add_section(own)
    acc2[...] = jnp.zeros(acc2.shape, F32)

    def wait_back(there, first, last):
        def body(i, _):
            s = there * PLANE + i
            back_copy(s, s, s).wait_recv()
            return 0

        lax.fori_loop(first, last, body, 0)

    def collect(there, first, many):
        at = [there * PLANE + first + i for i in range(many)]
        values = jnp.concatenate([returned[s] for s in at], 1)
        index = jnp.concatenate([lists[pl.ds(s, 1), :] for s in at], 1)
        top = values.astype(BF16)
        rest = (values - top.astype(F32)).astype(BF16)
        start = there * (PLANE * LANES) + first * LANES
        cols = pl.ds(pl.multiple_of(start, many * LANES), many * LANES)
        left = left2.at[:, 0 : many * LANES]
        scatter_block(index >> 8, hot2[:, cols], top, rest, left, acc2, count // 2)

    wait_back(plane, 0, inner)
    wait_back(plane, inner + 1, PLANE)
    collect(plane, 0, PLANE)
    near = own * per_section

    def collect_near(k, _):
        there = near + lax.rem(plane + k, per_section)
        wait_back(there, 0, PLANE)
        collect(there, 0, PLANE)
        return 0

    lax.fori_loop(1, per_section, collect_near, 0)
    def add_far(r, _):
        section = lax.rem(own + r, sections)
        lax.fori_loop(section * wide, (section + 1) * wide, wait_go, 0)
        add_section(section)
        return 0

    lax.fori_loop(1, sections, add_far, 0)

    for i in range(4):

        @pl.when(sends[i])
        def _(i=i):
            halo_copy(i).wait_send()

    def sent(k, _):
        d = lax.rem(me + k, tiles)
        rate_copy(me, d, d).wait_send()
        go_copy(me, d, d).wait_send()
        return 0

    lax.fori_loop(1, tiles, sent, 0)

    reverse = own < (sections + 1) // 2

    def far_back(k):
        return far_plane(jnp.where(reverse, planes - 1 + per_section - k, k))

    def collect_far(k, _):
        wait_back(far_back(k), 0, PLANE)
        collect(far_back(k), 0, PLANE)
        return 0

    lax.fori_loop(per_section, planes - 1, collect_far, 0)
    last = far_back(planes - 1)
    half = lax.div(lax.rem(inner + 1, PLANE), LAST)
    for part in range(PLANE // LAST):
        first = lax.rem(half + 1 + part, PLANE // LAST) * LAST
        wait_back(last, first, first + LAST)
        collect(last, first, LAST)

    def finish(k, _):
        d = lax.rem(me + k, tiles)
        back_copy(me, d, d).wait_send()
        return 0

    for j in range(count):
        total = acc_row(acc2, j)
        weight = total[species : species + 1]
        mixed = scaled[j, 0:species, :] * weight
        mean = total[:species] + mixed + fields[j, 0:species, :]
        out[pl.ds(j, species, stride=count), :] = mean * (1.0 / (weight + 1.0))

    lax.fori_loop(1, tiles, finish, 0)


def hand_over(first, second, first_out, second_out, sems):
    copies = [
        pltpu.make_async_copy(first, first_out, sems.at[0]),
        pltpu.make_async_copy(second, second_out, sems.at[1]),
    ]
    for copy in copies:
        copy.start()
    for copy in copies:
        copy.wait()


def on_device(
    cell_means, diffusion, mix_rate, send_lists, compositions, weights, particle_slots, partners
):
    species, rows_x, rows_y, depth = cell_means.shape
    count = rows_x * rows_y
    tiles = send_lists.shape[1]
    particles = compositions.shape[1]
    blocks = particles // LANES
    vmem = lambda *shape: pltpu.VMEM(shape, F32)
    half_vmem = lambda *shape: pltpu.VMEM(shape, BF16)
    operands = (
        cell_means.reshape(species * count, depth),
        diffusion.reshape(count, depth),
        mix_rate.reshape(count, depth),
        send_lists[0],
        compositions,
        weights.reshape(blocks, LANES),
        particle_slots.reshape(blocks, LANES),
        partners.reshape(blocks, LANES),
    )
    out, new = pl.pallas_call(
        functools.partial(
            whole_kernel, lax.axis_size("gx"), lax.axis_size("gy"), rows_x, rows_y
        ),
        out_shape=(
            pltpu.VMEM((species * count, LANES), F32),
            pltpu.VMEM((species, particles), F32),
        ),
        in_specs=[pl.BlockSpec(memory_space=pltpu.HBM)] * 8,
        out_specs=[pl.BlockSpec(memory_space=pltpu.VMEM)] * 2,
        name="whole_kernel",
        scratch_shapes=[pltpu.VMEM(a.shape, a.dtype) for a in operands]
        + [
            vmem(rows_x, rows_y, ROWS, LANES),
            vmem(4, max(rows_x, rows_y), ROWS, LANES),
            vmem(count, ROWS, LANES),
            vmem(count, ROWS, LANES),
            vmem(tiles, 1, LANES),
            vmem(tiles, 1, LANES),
            vmem(blocks, LANES),
            vmem(tiles, ROWS, LANES),
            vmem(tiles, ROWS, LANES),
            vmem(tiles, ROWS, LANES),
            vmem(tiles, ROWS, LANES),
            half_vmem(particles // 256 * ROWS, 512),
            vmem(particles // 256 * ROWS, WIDE),
            vmem(ROWS, particles),
            half_vmem(ROWS, particles),
            half_vmem(ROWS, particles),
            half_vmem(256, particles),
            half_vmem(256, tiles * LANES),
            half_vmem(2 * PLANE * ROWS, 1024),
            vmem(2 * PLANE * ROWS, 256),
            half_vmem(count // 2 * ROWS, 512),
            half_vmem(count * ROWS, PLANE * LANES),
            vmem(count * ROWS, 256),
            pltpu.SemaphoreType.DMA((8,)),
            pltpu.SemaphoreType.DMA((4,)),
            pltpu.SemaphoreType.DMA((4,)),
            pltpu.SemaphoreType.DMA((tiles,)),
            pltpu.SemaphoreType.DMA((tiles,)),
            pltpu.SemaphoreType.DMA((tiles,)),
            pltpu.SemaphoreType.DMA((tiles,)),
            pltpu.SemaphoreType.DMA((tiles,)),
            pltpu.SemaphoreType.DMA((tiles,)),
            pltpu.SemaphoreType.REGULAR,
        ],
        compiler_params=pltpu.CompilerParams(
            collective_id=0, has_side_effects=True, vmem_limit_bytes=63 * 1024 * 1024
        ),
    )(*operands)
    out, new = pl.pallas_call(
        hand_over,
        out_shape=tuple(jax.ShapeDtypeStruct(a.shape, a.dtype) for a in (out, new)),
        in_specs=[pl.BlockSpec(memory_space=pltpu.VMEM)] * 2,
        out_specs=[pl.BlockSpec(memory_space=pltpu.HBM)] * 2,
        scratch_shapes=[pltpu.SemaphoreType.DMA((2,))],
        compiler_params=pltpu.CompilerParams(vmem_limit_bytes=1024 * 1024),
        name="hand_over",
    )(out, new)
    return out.reshape(species, rows_x, rows_y, depth), new


def solution(mesh):
    in_specs = (
        P(None, "gx", "gy", None),
        P("gx", "gy", None),
        P("gx", "gy", None),
        P(("gx", "gy"), None, None),
        P(None, ("gx", "gy")),
        P(("gx", "gy")),
        P(("gx", "gy")),
        P(("gx", "gy")),
    )
    out_specs = (P(None, "gx", "gy", None), P(None, ("gx", "gy")))
    return jax.shard_map(
        on_device, mesh=mesh, in_specs=in_specs, out_specs=out_specs, check_vma=False
    )
```

```python
import functools

import jax
import jax.numpy as jnp
from jax import lax
from jax.experimental import pallas as pl
from jax.experimental.pallas import tpu as pltpu
from jax.sharding import PartitionSpec as P

PAIR_RATE = 0.3
LANES = 128
ROWS = 32
GROUPS = ROWS // 8
PLANE = 8
WIDE = 1024
FIRST = 0
LAST = 4
HALO_ROUNDS = 1
F32 = jnp.float32
BF16 = jnp.bfloat16


def select_group(index, parts, groups):
    group = jnp.broadcast_to(index >> 8, (ROWS, index.shape[1]))
    total = jnp.zeros(group.shape, F32)
    for h in range(groups):
        total = jnp.where(group == h, parts[h * ROWS : (h + 1) * ROWS, :], total)
    return total


def row_block(table, k, width):
    many = width // LANES
    return jnp.concatenate([table[pl.ds(k * many + i, 1), :] for i in range(many)], 1)


def inside(cells, diffusion, fields, rows_x, rows_y):
    lane = lax.broadcasted_iota(jnp.int32, (ROWS, LANES), 1)
    for x in range(rows_x):
        for y in range(rows_y):
            mid = cells[x, y]
            total = jnp.where(lane < LANES - 1, pltpu.roll(mid, LANES - 1, 1), 0.0)
            total = total + jnp.where(lane > 0, pltpu.roll(mid, 1, 1), 0.0)
            for other in ((x + 1, y), (x - 1, y), (x, y + 1), (x, y - 1)):
                if 0 <= other[0] < rows_x and 0 <= other[1] < rows_y:
                    total = total + cells[other[0], other[1]]
            j = x * rows_y + y
            fields[j] = mid + diffusion[j : j + 1, :] * (total - 6.0 * mid)


def rim(halo, diffusion, fields, blend, scaled, table, rows_x, rows_y):
    for x in range(rows_x):
        for y in range(rows_y):
            j = x * rows_y + y
            outer = [halo[1, y]] if x + 1 == rows_x else []
            outer += [halo[0, y]] if x == 0 else []
            outer += [halo[3, x]] if y + 1 == rows_y else []
            outer += [halo[2, x]] if y == 0 else []
            filtered = fields[j]
            if outer:
                filtered = filtered + diffusion[j : j + 1, :] * sum(outer[1:], outer[0])
                fields[j] = filtered
            mixed = filtered * blend[j : j + 1, :]
            scaled[j] = mixed
            first = mixed.astype(BF16)
            rows = slice(j // 2 * ROWS, (j // 2 + 1) * ROWS)
            at = j % 2 * LANES
            table[rows, at : at + LANES] = first
            table[rows, 256 + at : 256 + at + LANES] = (mixed - first.astype(F32)).astype(BF16)


def scatter_block(group, hot, high, low, left, acc, groups):
    width = group.shape[1]
    group = jnp.broadcast_to(group.astype(F32).astype(BF16), (ROWS, width))
    for g in range(groups):
        mask = group == jnp.array(g, BF16)
        zero = jnp.zeros((ROWS, width), BF16)
        left[2 * g * ROWS : (2 * g + 1) * ROWS, :] = jnp.where(mask, high, zero)
        left[(2 * g + 1) * ROWS : (2 * g + 2) * ROWS, :] = jnp.where(mask, low, zero)
    acc[...] += lax.dot_general(
        left[...], hot, (((1,), (1,)), ((), ())), preferred_element_type=F32
    )


def hot_rows(index):
    place = lax.broadcasted_iota(jnp.int32, (256, index.shape[1]), 0)
    return jnp.where(place == (index & 255), 1.0, 0.0).astype(BF16)


def acc_row(acc, j):
    g, half = j // 2, (j % 2) * LANES
    return (
        acc[2 * g * ROWS : (2 * g + 1) * ROWS, half : half + LANES]
        + acc[(2 * g + 1) * ROWS : (2 * g + 2) * ROWS, half : half + LANES]
    )


def load_cells(means, cells, rows_x, rows_y):
    species = means.shape[0] // (rows_x * rows_y)
    for x in range(rows_x):
        for y in range(rows_y):
            j = x * rows_y + y
            cells[x, y, 0:species, :] = means[pl.ds(j, species, stride=rows_x * rows_y), :]
            cells[x, y, species:ROWS, :] = jnp.zeros((ROWS - species, LANES), F32)


def split_table(compositions, table):
    species, particles = compositions.shape
    for h in range(particles // 256):
        values = compositions[:, h * 256 : (h + 1) * 256]
        values = jnp.concatenate([values, jnp.zeros((ROWS - species, 256), F32)], 0)
        first = values.astype(BF16)
        table[h * ROWS : (h + 1) * ROWS, 0:256] = first
        table[h * ROWS : (h + 1) * ROWS, 256:512] = (values - first.astype(F32)).astype(BF16)


def gather_pairs(compositions, partners, table, parts, pair, first, last):
    species, particles = compositions.shape

    def body(k, _):
        index = row_block(partners, k, WIDE)
        hot = hot_rows(index)
        parts[...] = jnp.dot(
            table[...], jnp.concatenate([hot, hot], 0), preferred_element_type=F32
        )
        total = select_group(index, parts, particles // 256)
        at = pl.ds(pl.multiple_of(k * WIDE, WIDE), WIDE)
        pair[0:species, at] = PAIR_RATE * (compositions[:, at] - total[:species])
        return 0

    lax.fori_loop(first, last, body, 0)


def pick_rates(lists, rates, buffer):
    tiles = lists.shape[0]
    for first in range(0, tiles, 8):
        index = lists[first : first + 8, :]
        lane, chunk = index & (LANES - 1), index >> 7
        total = jnp.zeros((8, LANES), F32)
        for j in range(rates.shape[0]):
            row = jnp.broadcast_to(rates[j : j + 1, :], (8, LANES))
            found = jnp.take_along_axis(row, lane, axis=1, mode="promise_in_bounds")
            total = jnp.where(chunk == j, found, total)
        for i in range(8):
            buffer[first + i] = total[i : i + 1, :]


def spread_rates(slots, rates, out):
    blocks = slots.shape[0]
    parts = range(0, blocks, 8)
    lanes = [slots[b : b + 8, :] & (LANES - 1) for b in parts]
    chunks = [slots[b : b + 8, :] >> 7 for b in parts]

    def step(s, totals):
        row = jnp.broadcast_to(rates[s], (8, LANES))
        return tuple(
            jnp.where(
                chunk == s,
                jnp.take_along_axis(row, lane, axis=1, mode="promise_in_bounds"),
                total,
            )
            for lane, chunk, total in zip(lanes, chunks, totals)
        )

    start = tuple(jnp.zeros((8, LANES), F32) for _ in parts)
    totals = lax.fori_loop(0, rates.shape[0], step, start, unroll=8)
    for b, total in zip(parts, totals):
        out[b : b + 8, :] = total


def add_fields(received, slots, hot, table, parts, new, section, groups):
    species, particles = new.shape
    for h in range(groups):
        s = 2 * (section * groups + h)
        values = jnp.concatenate([received[s], received[s + 1]], 1)
        first = values.astype(BF16)
        rows = slice(h * ROWS, (h + 1) * ROWS)
        table[rows, 0:256] = first
        table[rows, 256:512] = (values - first.astype(F32)).astype(BF16)

    def body(k, _):
        at = pl.ds(pl.multiple_of(k * WIDE, WIDE), WIDE)
        both = hot[:, at]
        parts[0 : groups * ROWS, :] = jnp.dot(
            table[0 : groups * ROWS, :],
            jnp.concatenate([both, both], 0),
            preferred_element_type=F32,
        )
        index = row_block(slots, k, WIDE) - section * (groups * 256)
        new[:, at] += select_group(index, parts, groups)[:species]
        return 0

    lax.fori_loop(0, particles // WIDE, body, 0)


def whole_kernel(
    nx, ny, rows_x, rows_y, *refs
):
    inputs, (out, new), refs = refs[:8], refs[8:10], refs[10:]
    staged, refs = refs[:8], refs[8:]
    means, diffusion, rate, lists, compositions, weights, slots, partners = staged
    (
        cells, halo, fields, scaled, rates_out, rates_in, rates, outgoing, received, moments,
        returned, table, parts, pair, high, low, hot1, hot2, left1, acc1, field_table, left2, acc2,
        in_sems, halo_send, halo_recv, rate_send, rate_recv, go_send, go_recv,
        back_send, back_recv, late,
    ) = refs
    tiles = nx * ny
    planes = tiles // PLANE
    count = rows_x * rows_y
    species = compositions.shape[0]
    blocks = slots.shape[0]
    gx, gy = lax.axis_index("gx"), lax.axis_index("gy")
    me = gx * ny + gy
    plane, inner = lax.div(me, PLANE), lax.rem(me, PLANE)

    def place(d):
        return (lax.div(d, ny), lax.rem(d, ny))

    loads = [
        pltpu.make_async_copy(inputs[i], staged[i], in_sems.at[i]) for i in range(8)
    ]
    for i in (0, 4, 7, 2, 3, 6, 1, 5):
        loads[i].start()

    barrier = pltpu.get_barrier_semaphore()

    def signal(semaphore, d):
        pl.semaphore_signal(
            semaphore, inc=1, device_id=place(d), device_id_type=pl.DeviceIdType.MESH
        )

    def greet_plane(k, _):
        signal(barrier, plane * PLANE + lax.rem(inner + k, PLANE))
        return 0

    def greet(d, _):
        signal(barrier, d)
        return 0

    def announce(d, _):
        signal(late, d)
        return 0

    lax.fori_loop(1, PLANE, greet_plane, 0)
    above = jnp.logical_and(gx < nx - 1, lax.div(me + ny, PLANE) > plane)
    below = jnp.logical_and(gx > 0, lax.div(me - ny + tiles, PLANE) < plane + planes)

    @pl.when(below)
    def _():
        signal(barrier, me - ny)

    lax.fori_loop((plane + 1) * PLANE, tiles, greet, 0)

    loads[0].wait()
    for x in range(rows_x):
        for y in range(rows_y):
            j = x * rows_y + y
            cells[x, y, 0:species, :] = means[pl.ds(j, species, stride=count), :]
            cells[x, y, species:ROWS, :] = jnp.zeros((ROWS - species, LANES), F32)

    pl.semaphore_wait(barrier, (plane + 1) * PLANE - 1 + above.astype(jnp.int32))

    def halo_copy(i):
        source, length, target = (
            (cells.at[rows_x - 1, :, 0:species], rows_y, (gx + 1, gy)),
            (cells.at[0, :, 0:species], rows_y, (gx - 1, gy)),
            (cells.at[:, rows_y - 1, 0:species], rows_x, (gx, gy + 1)),
            (cells.at[:, 0, 0:species], rows_x, (gx, gy - 1)),
        )[i]
        return pltpu.make_async_remote_copy(
            src_ref=source,
            dst_ref=halo.at[i, 0:length, 0:species],
            send_sem=halo_send.at[i],
            recv_sem=halo_recv.at[i],
            device_id=target,
            device_id_type=pl.DeviceIdType.MESH,
        )

    sends = (gx < nx - 1, gx > 0, gy < ny - 1, gy > 0)
    receives = (gx > 0, gx < nx - 1, gy > 0, gy < ny - 1)
    for i in (2, 3, 0, 1):

        @pl.when(sends[i])
        def _(i=i):
            halo_copy(i).start()

    lax.fori_loop(0, plane * PLANE, announce, 0)
    for i in range(4):
        halo[i, :, species:ROWS] = jnp.zeros(halo[i, :, species:ROWS].shape, F32)

        @pl.when(jnp.logical_not(receives[i]))
        def _(i=i):
            halo[i, :, 0:species] = jnp.zeros(halo[i, :, 0:species].shape, F32)

    rounds = blocks * LANES // WIDE
    hops = lax.div(gx, 2) + lax.rem(gx, 2) + lax.div(gy, 2)
    early = jnp.where(hops == 0, FIRST, 0)
    early = jnp.minimum(early, rounds)
    soon = jnp.minimum(early + HALO_ROUNDS, rounds)
    loads[4].wait()
    loads[7].wait()
    split_table(compositions, table)
    gather_pairs(compositions, partners, table, parts, pair, 0, early)

    loads[2].wait()
    loads[3].wait()
    blend = 1.0 - jnp.exp(-rate[...])
    pick_rates(lists, blend, rates_out)
    rates_in[me] = rates_out[me]

    def rate_copy(source, d, target):
        return pltpu.make_async_remote_copy(
            src_ref=rates_out.at[d],
            dst_ref=rates_in.at[source],
            send_sem=rate_send.at[d],
            recv_sem=rate_recv.at[source],
            device_id=place(target),
            device_id_type=pl.DeviceIdType.MESH,
        )

    def send_rates(k, _):
        d = lax.rem(me + k, tiles)
        rate_copy(me, d, d).start()
        return 0


    loads[6].wait()
    for b in range(0, blocks, 4):
        hot1[:, b * LANES : (b + 4) * LANES] = hot_rows(row_block(slots, b // 4, 4 * LANES))
    for b in range(0, tiles, 4):
        hot2[:, b * LANES : (b + 4) * LANES] = hot_rows(row_block(lists, b // 4, 4 * LANES))
    loads[1].wait()
    inside(cells, diffusion, fields, rows_x, rows_y)
    gather_pairs(compositions, partners, table, parts, pair, early, soon)

    @pl.when(plane < planes - 1)
    def _():
        pl.semaphore_wait(late, tiles - (plane + 1) * PLANE)

    lax.fori_loop(1, tiles, send_rates, 0)

    def go_copy(source, d, target):
        return pltpu.make_async_remote_copy(
            src_ref=outgoing.at[d, 0:species],
            dst_ref=received.at[source, 0:species],
            send_sem=go_send.at[d],
            recv_sem=go_recv.at[source],
            device_id=place(target),
            device_id_type=pl.DeviceIdType.MESH,
        )

    def back_copy(source, d, target):
        return pltpu.make_async_remote_copy(
            src_ref=moments.at[d, 0 : species + 1],
            dst_ref=returned.at[source, 0 : species + 1],
            send_sem=back_send.at[d],
            recv_sem=back_recv.at[source],
            device_id=place(target),
            device_id_type=pl.DeviceIdType.MESH,
        )

    wide = acc1.shape[0] // ROWS
    sections = tiles // wide
    own = lax.div(me, wide)
    per_section = wide // PLANE

    def peer(section, k):
        turn = lax.div(k, PLANE)
        near = lax.rem(plane + 1 + turn, per_section)
        turn = jnp.where(section == own, near, turn)
        return section * wide + turn * PLANE + lax.rem(inner + k, PLANE)

    def fill(there):
        at = pl.ds(pl.multiple_of(there * (PLANE * LANES), PLANE * LANES), PLANE * LANES)
        hot = hot2[:, at]
        parts[0 : count // 2 * ROWS, :] = jnp.dot(
            field_table[...], jnp.concatenate([hot, hot], 0), preferred_element_type=F32
        )
        index = row_block(lists, there, PLANE * LANES)
        found = select_group(index, parts, count // 2)
        for i in range(PLANE):
            outgoing[there * PLANE + i] = found[:, i * LANES : (i + 1) * LANES]

    def send_go(there, first):
        def body(k, _):
            d = there * PLANE + lax.rem(inner + k, PLANE)
            go_copy(me, d, d).start()
            return 0

        lax.fori_loop(first, PLANE, body, 0)

    def far_plane(k):
        return lax.rem(own * per_section + k, planes)

    for i in range(4):

        @pl.when(receives[i])
        def _(i=i):
            halo_copy(i).wait_recv()

    rim(halo, diffusion, fields, blend, scaled, field_table, rows_x, rows_y)

    def go_far(k, _):
        fill(far_plane(k))
        send_go(far_plane(k), 0)
        return 0

    lax.fori_loop(per_section, planes - 1, go_far, 0)
    gather_pairs(compositions, partners, table, parts, pair, soon, rounds)
    lax.fori_loop(planes - 1, planes, go_far, 0)
    def go_near(k, _):
        there = own * per_section + lax.rem(plane + k, per_section)
        fill(there)
        send_go(there, 0)
        return 0

    lax.fori_loop(1, per_section, go_near, 0)
    fill(plane)
    received[me] = outgoing[me]
    send_go(plane, 1)
    loads[5].wait()

    def wait_rates(k, _):
        s = lax.rem(me + k, tiles)
        rate_copy(s, s, s).wait_recv()
        return 0

    lax.fori_loop(1, tiles, wait_rates, 0)
    spread_rates(slots, rates_in, rates)

    def weigh(b, _):
        at = pl.ds(pl.multiple_of(b * LANES, LANES), LANES)
        mine = compositions[:, at]
        fresh = mine - rates[pl.ds(b, 1), :] * mine - pair[0:species, at]
        new[:, at] = fresh
        weight = weights[pl.ds(b, 1), :]
        values = jnp.concatenate(
            [weight * fresh, weight, jnp.zeros((ROWS - species - 1, LANES), F32)], 0
        )
        top = values.astype(BF16)
        high[:, at] = top
        low[:, at] = (values - top.astype(F32)).astype(BF16)
        return 0

    lax.fori_loop(0, blocks, weigh, 0, unroll=4)

    per = left1.shape[1]

    def sum_slots(section):
        acc1[...] = jnp.zeros(acc1.shape, F32)

        def scatter(k, _):
            group = (row_block(slots, k, per) >> 8) - section * (wide // 2)
            cols = pl.ds(pl.multiple_of(k * per, per), per)
            scatter_block(
                group, hot1[:, cols], high[:, cols], low[:, cols], left1, acc1, wide // 2
            )
            return 0

        lax.fori_loop(0, blocks * LANES // per, scatter, 0)
        for i in range(wide):
            moments[section * wide + i] = acc_row(acc1, i)

    def send_back(section, first, last):
        def body(k, _):
            d = peer(section, k)
            back_copy(me, d, d).start()
            return 0

        lax.fori_loop(first, last, body, 0)

    def other(r, _):
        section = lax.rem(own + r, sections)
        sum_slots(section)
        send_back(section, 0, wide)
        return 0

    lax.fori_loop(1, sections, other, 0)

    sum_slots(own)
    send_back(own, 0, wide - PLANE)
    send_back(own, wide - PLANE + 1, wide)
    returned[me] = moments[me]

    def wait_go(s, _):
        go_copy(s, s, s).wait_recv()
        return 0

    def add_section(section):
        add_fields(received, slots, hot1, table, parts, new, section, wide // 2)

    lax.fori_loop(own * wide, me, wait_go, 0)
    lax.fori_loop(me + 1, (own + 1) * wide, wait_go, 0)
    add_section(own)
    acc2[...] = jnp.zeros(acc2.shape, F32)

    def wait_back(there, first, last):
        def body(i, _):
            s = there * PLANE + i
            back_copy(s, s, s).wait_recv()
            return 0

        lax.fori_loop(first, last, body, 0)

    def collect(there, first, many):
        at = [there * PLANE + first + i for i in range(many)]
        values = jnp.concatenate([returned[s] for s in at], 1)
        index = jnp.concatenate([lists[pl.ds(s, 1), :] for s in at], 1)
        top = values.astype(BF16)
        rest = (values - top.astype(F32)).astype(BF16)
        start = there * (PLANE * LANES) + first * LANES
        cols = pl.ds(pl.multiple_of(start, many * LANES), many * LANES)
        left = left2.at[:, 0 : many * LANES]
        scatter_block(index >> 8, hot2[:, cols], top, rest, left, acc2, count // 2)

    wait_back(plane, 0, inner)
    wait_back(plane, inner + 1, PLANE)
    collect(plane, 0, PLANE)
    near = own * per_section

    def collect_near(k, _):
        there = near + lax.rem(plane + k, per_section)
        wait_back(there, 0, PLANE)
        collect(there, 0, PLANE)
        return 0

    lax.fori_loop(1, per_section, collect_near, 0)
    def add_far(r, _):
        section = lax.rem(own + r, sections)
        lax.fori_loop(section * wide, (section + 1) * wide, wait_go, 0)
        add_section(section)
        return 0

    lax.fori_loop(1, sections, add_far, 0)

    for i in range(4):

        @pl.when(sends[i])
        def _(i=i):
            halo_copy(i).wait_send()

    def sent(k, _):
        d = lax.rem(me + k, tiles)
        rate_copy(me, d, d).wait_send()
        go_copy(me, d, d).wait_send()
        return 0

    lax.fori_loop(1, tiles, sent, 0)

    reverse = own < (sections + 1) // 2

    def far_back(k):
        return far_plane(jnp.where(reverse, planes - 1 + per_section - k, k))

    def collect_far(k, _):
        wait_back(far_back(k), 0, PLANE)
        collect(far_back(k), 0, PLANE)
        return 0

    lax.fori_loop(per_section, planes - 1, collect_far, 0)
    last = far_back(planes - 1)
    half = lax.div(lax.rem(inner + 1, PLANE), LAST)

    def finish(d, _):
        back_copy(me, d, d).wait_send()
        return 0

    def finish_plane(there):
        lax.fori_loop(there * PLANE, (there + 1) * PLANE, finish, 0)

    def finish_far(k, _):
        finish_plane(far_plane(k))
        return 0

    lax.fori_loop(per_section, planes - 1, finish_far, 0)
    lax.fori_loop(own * wide, me, finish, 0)
    lax.fori_loop(me + 1, (own + 1) * wide, finish, 0)
    for part in range(PLANE // LAST):
        first = lax.rem(half + 1 + part, PLANE // LAST) * LAST
        wait_back(last, first, first + LAST)
        collect(last, first, LAST)

    for j in range(count):
        total = acc_row(acc2, j)
        weight = total[species : species + 1]
        mixed = scaled[j, 0:species, :] * weight
        mean = total[:species] + mixed + fields[j, 0:species, :]
        out[pl.ds(j, species, stride=count), :] = mean * (1.0 / (weight + 1.0))

    finish_plane(far_plane(planes - 1))


def hand_over(first, second, first_out, second_out, sems):
    copies = [
        pltpu.make_async_copy(first, first_out, sems.at[0]),
        pltpu.make_async_copy(second, second_out, sems.at[1]),
    ]
    for copy in copies:
        copy.start()
    for copy in copies:
        copy.wait()


def on_device(
    cell_means, diffusion, mix_rate, send_lists, compositions, weights, particle_slots, partners
):
    species, rows_x, rows_y, depth = cell_means.shape
    count = rows_x * rows_y
    tiles = send_lists.shape[1]
    particles = compositions.shape[1]
    blocks = particles // LANES
    vmem = lambda *shape: pltpu.VMEM(shape, F32)
    half_vmem = lambda *shape: pltpu.VMEM(shape, BF16)
    operands = (
        cell_means.reshape(species * count, depth),
        diffusion.reshape(count, depth),
        mix_rate.reshape(count, depth),
        send_lists[0],
        compositions,
        weights.reshape(blocks, LANES),
        particle_slots.reshape(blocks, LANES),
        partners.reshape(blocks, LANES),
    )
    out, new = pl.pallas_call(
        functools.partial(
            whole_kernel, lax.axis_size("gx"), lax.axis_size("gy"), rows_x, rows_y
        ),
        out_shape=(
            pltpu.VMEM((species * count, LANES), F32),
            pltpu.VMEM((species, particles), F32),
        ),
        in_specs=[pl.BlockSpec(memory_space=pltpu.HBM)] * 8,
        out_specs=[pl.BlockSpec(memory_space=pltpu.VMEM)] * 2,
        name="whole_kernel",
        scratch_shapes=[pltpu.VMEM(a.shape, a.dtype) for a in operands]
        + [
            vmem(rows_x, rows_y, ROWS, LANES),
            vmem(4, max(rows_x, rows_y), ROWS, LANES),
            vmem(count, ROWS, LANES),
            vmem(count, ROWS, LANES),
            vmem(tiles, 1, LANES),
            vmem(tiles, 1, LANES),
            vmem(blocks, LANES),
            vmem(tiles, ROWS, LANES),
            vmem(tiles, ROWS, LANES),
            vmem(tiles, ROWS, LANES),
            vmem(tiles, ROWS, LANES),
            half_vmem(particles // 256 * ROWS, 512),
            vmem(particles // 256 * ROWS, WIDE),
            vmem(ROWS, particles),
            half_vmem(ROWS, particles),
            half_vmem(ROWS, particles),
            half_vmem(256, particles),
            half_vmem(256, tiles * LANES),
            half_vmem(2 * PLANE * ROWS, 1024),
            vmem(2 * PLANE * ROWS, 256),
            half_vmem(count // 2 * ROWS, 512),
            half_vmem(count * ROWS, PLANE * LANES),
            vmem(count * ROWS, 256),
            pltpu.SemaphoreType.DMA((8,)),
            pltpu.SemaphoreType.DMA((4,)),
            pltpu.SemaphoreType.DMA((4,)),
            pltpu.SemaphoreType.DMA((tiles,)),
            pltpu.SemaphoreType.DMA((tiles,)),
            pltpu.SemaphoreType.DMA((tiles,)),
            pltpu.SemaphoreType.DMA((tiles,)),
            pltpu.SemaphoreType.DMA((tiles,)),
            pltpu.SemaphoreType.DMA((tiles,)),
            pltpu.SemaphoreType.REGULAR,
        ],
        compiler_params=pltpu.CompilerParams(
            collective_id=0, has_side_effects=True, vmem_limit_bytes=63 * 1024 * 1024
        ),
    )(*operands)
    out, new = pl.pallas_call(
        hand_over,
        out_shape=tuple(jax.ShapeDtypeStruct(a.shape, a.dtype) for a in (out, new)),
        in_specs=[pl.BlockSpec(memory_space=pltpu.VMEM)] * 2,
        out_specs=[pl.BlockSpec(memory_space=pltpu.HBM)] * 2,
        scratch_shapes=[pltpu.SemaphoreType.DMA((2,))],
        compiler_params=pltpu.CompilerParams(vmem_limit_bytes=1024 * 1024),
        name="hand_over",
    )(out, new)
    return out.reshape(species, rows_x, rows_y, depth), new


def solution(mesh):
    in_specs = (
        P(None, "gx", "gy", None),
        P("gx", "gy", None),
        P("gx", "gy", None),
        P(("gx", "gy"), None, None),
        P(None, ("gx", "gy")),
        P(("gx", "gy")),
        P(("gx", "gy")),
        P(("gx", "gy")),
    )
    out_specs = (P(None, "gx", "gy", None), P(None, ("gx", "gy")))
    return jax.shard_map(
        on_device, mesh=mesh, in_specs=in_specs, out_specs=out_specs, check_vma=False
    )
```

```python
import functools

import jax
import jax.numpy as jnp
from jax import lax
from jax.experimental import pallas as pl
from jax.experimental.pallas import tpu as pltpu
from jax.sharding import PartitionSpec as P

PAIR_RATE = 0.3
LANES = 128
ROWS = 32
GROUPS = ROWS // 8
PLANE = 8
WIDE = 1024
FIRST = 0
LAST = 4
HALO_ROUNDS = 1
F32 = jnp.float32
BF16 = jnp.bfloat16


def select_group(index, parts, groups):
    group = jnp.broadcast_to(index >> 8, (ROWS, index.shape[1]))
    total = jnp.zeros(group.shape, F32)
    for h in range(groups):
        total = jnp.where(group == h, parts[h * ROWS : (h + 1) * ROWS, :], total)
    return total


def row_block(table, k, width):
    many = width // LANES
    return jnp.concatenate([table[pl.ds(k * many + i, 1), :] for i in range(many)], 1)


def inside(cells, diffusion, fields, rows_x, rows_y):
    lane = lax.broadcasted_iota(jnp.int32, (ROWS, LANES), 1)
    for x in range(rows_x):
        for y in range(rows_y):
            mid = cells[x, y]
            total = jnp.where(lane < LANES - 1, pltpu.roll(mid, LANES - 1, 1), 0.0)
            total = total + jnp.where(lane > 0, pltpu.roll(mid, 1, 1), 0.0)
            for other in ((x + 1, y), (x - 1, y), (x, y + 1), (x, y - 1)):
                if 0 <= other[0] < rows_x and 0 <= other[1] < rows_y:
                    total = total + cells[other[0], other[1]]
            j = x * rows_y + y
            fields[j] = mid + diffusion[j : j + 1, :] * (total - 6.0 * mid)


def rim(halo, diffusion, fields, blend, table, rows_x, rows_y):
    for x in range(rows_x):
        for y in range(rows_y):
            j = x * rows_y + y
            outer = [halo[1, y]] if x + 1 == rows_x else []
            outer += [halo[0, y]] if x == 0 else []
            outer += [halo[3, x]] if y + 1 == rows_y else []
            outer += [halo[2, x]] if y == 0 else []
            filtered = fields[j]
            if outer:
                filtered = filtered + diffusion[j : j + 1, :] * sum(outer[1:], outer[0])
                fields[j] = filtered
            mixed = filtered * blend[j : j + 1, :]
            first = mixed.astype(BF16)
            rows = slice(j // 2 * ROWS, (j // 2 + 1) * ROWS)
            at = j % 2 * LANES
            table[rows, at : at + LANES] = first
            table[rows, 256 + at : 256 + at + LANES] = (mixed - first.astype(F32)).astype(BF16)


def scatter_block(group, hot, high, low, left, acc, groups):
    width = group.shape[1]
    group = jnp.broadcast_to(group.astype(F32).astype(BF16), (ROWS, width))
    for g in range(groups):
        mask = group == jnp.array(g, BF16)
        zero = jnp.zeros((ROWS, width), BF16)
        left[2 * g * ROWS : (2 * g + 1) * ROWS, :] = jnp.where(mask, high, zero)
        left[(2 * g + 1) * ROWS : (2 * g + 2) * ROWS, :] = jnp.where(mask, low, zero)
    acc[...] += lax.dot_general(
        left[...], hot, (((1,), (1,)), ((), ())), preferred_element_type=F32
    )


def hot_rows(index):
    place = lax.broadcasted_iota(jnp.int32, (256, index.shape[1]), 0)
    return jnp.where(place == (index & 255), 1.0, 0.0).astype(BF16)


def acc_row(acc, j):
    g, half = j // 2, (j % 2) * LANES
    return (
        acc[2 * g * ROWS : (2 * g + 1) * ROWS, half : half + LANES]
        + acc[(2 * g + 1) * ROWS : (2 * g + 2) * ROWS, half : half + LANES]
    )


def load_cells(means, cells, rows_x, rows_y):
    species = means.shape[0] // (rows_x * rows_y)
    for x in range(rows_x):
        for y in range(rows_y):
            j = x * rows_y + y
            cells[x, y, 0:species, :] = means[pl.ds(j, species, stride=rows_x * rows_y), :]
            cells[x, y, species:ROWS, :] = jnp.zeros((ROWS - species, LANES), F32)


def split_table(compositions, table):
    species, particles = compositions.shape
    for h in range(particles // 256):
        values = compositions[:, h * 256 : (h + 1) * 256]
        values = jnp.concatenate([values, jnp.zeros((ROWS - species, 256), F32)], 0)
        first = values.astype(BF16)
        table[h * ROWS : (h + 1) * ROWS, 0:256] = first
        table[h * ROWS : (h + 1) * ROWS, 256:512] = (values - first.astype(F32)).astype(BF16)


def gather_pairs(compositions, partners, table, parts, pair, first, last):
    species, particles = compositions.shape

    def body(k, _):
        index = row_block(partners, k, WIDE)
        hot = hot_rows(index)
        parts[...] = jnp.dot(
            table[...], jnp.concatenate([hot, hot], 0), preferred_element_type=F32
        )
        total = select_group(index, parts, particles // 256)
        at = pl.ds(pl.multiple_of(k * WIDE, WIDE), WIDE)
        pair[0:species, at] = PAIR_RATE * (compositions[:, at] - total[:species])
        return 0

    lax.fori_loop(first, last, body, 0)


def pick_rates(lists, rates, buffer):
    tiles = lists.shape[0]
    for first in range(0, tiles, 8):
        index = lists[first : first + 8, :]
        lane, chunk = index & (LANES - 1), index >> 7
        total = jnp.zeros((8, LANES), F32)
        for j in range(rates.shape[0]):
            row = jnp.broadcast_to(rates[j : j + 1, :], (8, LANES))
            found = jnp.take_along_axis(row, lane, axis=1, mode="promise_in_bounds")
            total = jnp.where(chunk == j, found, total)
        for i in range(8):
            buffer[first + i] = total[i : i + 1, :]


def spread_rates(slots, rates, out):
    blocks = slots.shape[0]
    parts = range(0, blocks, 8)
    lanes = [slots[b : b + 8, :] & (LANES - 1) for b in parts]
    chunks = [slots[b : b + 8, :] >> 7 for b in parts]

    def step(s, totals):
        row = jnp.broadcast_to(rates[s], (8, LANES))
        return tuple(
            jnp.where(
                chunk == s,
                jnp.take_along_axis(row, lane, axis=1, mode="promise_in_bounds"),
                total,
            )
            for lane, chunk, total in zip(lanes, chunks, totals)
        )

    start = tuple(jnp.zeros((8, LANES), F32) for _ in parts)
    totals = lax.fori_loop(0, rates.shape[0], step, start, unroll=8)
    for b, total in zip(parts, totals):
        out[b : b + 8, :] = total


def add_fields(received, slots, hot, table, parts, new, section, groups):
    species, particles = new.shape
    for h in range(groups):
        s = 2 * (section * groups + h)
        values = jnp.concatenate([received[s], received[s + 1]], 1)
        first = values.astype(BF16)
        rows = slice(h * ROWS, (h + 1) * ROWS)
        table[rows, 0:256] = first
        table[rows, 256:512] = (values - first.astype(F32)).astype(BF16)

    def body(k, _):
        at = pl.ds(pl.multiple_of(k * WIDE, WIDE), WIDE)
        both = hot[:, at]
        parts[0 : groups * ROWS, :] = jnp.dot(
            table[0 : groups * ROWS, :],
            jnp.concatenate([both, both], 0),
            preferred_element_type=F32,
        )
        index = row_block(slots, k, WIDE) - section * (groups * 256)
        new[:, at] += select_group(index, parts, groups)[:species]
        return 0

    lax.fori_loop(0, particles // WIDE, body, 0)


def whole_kernel(
    nx, ny, rows_x, rows_y, *refs
):
    inputs, (out, new), refs = refs[:8], refs[8:10], refs[10:]
    staged, refs = refs[:8], refs[8:]
    means, diffusion, rate, lists, compositions, weights, slots, partners = staged
    (
        cells, halo, fields, rates_out, rates_in, rates, outgoing, received, moments,
        returned, table, parts, pair, high, low, hot1, hot2, left1, acc1, field_table, left2, acc2,
        in_sems, halo_send, halo_recv, rate_send, rate_recv, go_send, go_recv,
        back_send, back_recv, late,
    ) = refs
    tiles = nx * ny
    planes = tiles // PLANE
    count = rows_x * rows_y
    species = compositions.shape[0]
    blocks = slots.shape[0]
    gx, gy = lax.axis_index("gx"), lax.axis_index("gy")
    me = gx * ny + gy
    plane, inner = lax.div(me, PLANE), lax.rem(me, PLANE)

    def place(d):
        return (lax.div(d, ny), lax.rem(d, ny))

    loads = [
        pltpu.make_async_copy(inputs[i], staged[i], in_sems.at[i]) for i in range(8)
    ]
    for i in (0, 4, 7, 2, 3, 6, 1, 5):
        loads[i].start()

    barrier = pltpu.get_barrier_semaphore()

    def signal(semaphore, d):
        pl.semaphore_signal(
            semaphore, inc=1, device_id=place(d), device_id_type=pl.DeviceIdType.MESH
        )

    def greet_plane(k, _):
        signal(barrier, plane * PLANE + lax.rem(inner + k, PLANE))
        return 0

    def greet(d, _):
        signal(barrier, d)
        return 0

    def announce(d, _):
        signal(late, d)
        return 0

    lax.fori_loop(1, PLANE, greet_plane, 0)
    above = jnp.logical_and(gx < nx - 1, lax.div(me + ny, PLANE) > plane)
    below = jnp.logical_and(gx > 0, lax.div(me - ny + tiles, PLANE) < plane + planes)

    @pl.when(below)
    def _():
        signal(barrier, me - ny)

    lax.fori_loop((plane + 1) * PLANE, tiles, greet, 0)

    loads[0].wait()
    for x in range(rows_x):
        for y in range(rows_y):
            j = x * rows_y + y
            cells[x, y, 0:species, :] = means[pl.ds(j, species, stride=count), :]
            cells[x, y, species:ROWS, :] = jnp.zeros((ROWS - species, LANES), F32)

    pl.semaphore_wait(barrier, (plane + 1) * PLANE - 1 + above.astype(jnp.int32))

    def halo_copy(i):
        source, length, target = (
            (cells.at[rows_x - 1, :, 0:species], rows_y, (gx + 1, gy)),
            (cells.at[0, :, 0:species], rows_y, (gx - 1, gy)),
            (cells.at[:, rows_y - 1, 0:species], rows_x, (gx, gy + 1)),
            (cells.at[:, 0, 0:species], rows_x, (gx, gy - 1)),
        )[i]
        return pltpu.make_async_remote_copy(
            src_ref=source,
            dst_ref=halo.at[i, 0:length, 0:species],
            send_sem=halo_send.at[i],
            recv_sem=halo_recv.at[i],
            device_id=target,
            device_id_type=pl.DeviceIdType.MESH,
        )

    sends = (gx < nx - 1, gx > 0, gy < ny - 1, gy > 0)
    receives = (gx > 0, gx < nx - 1, gy > 0, gy < ny - 1)
    for i in (2, 3, 0, 1):

        @pl.when(sends[i])
        def _(i=i):
            halo_copy(i).start()

    lax.fori_loop(0, plane * PLANE, announce, 0)
    for i in range(4):
        halo[i, :, species:ROWS] = jnp.zeros(halo[i, :, species:ROWS].shape, F32)

        @pl.when(jnp.logical_not(receives[i]))
        def _(i=i):
            halo[i, :, 0:species] = jnp.zeros(halo[i, :, 0:species].shape, F32)

    rounds = blocks * LANES // WIDE
    hops = lax.div(gx, 2) + lax.rem(gx, 2) + lax.div(gy, 2)
    early = jnp.where(hops == 0, FIRST, 0)
    early = jnp.minimum(early, rounds)
    soon = jnp.minimum(early + HALO_ROUNDS, rounds)
    loads[4].wait()
    loads[7].wait()
    split_table(compositions, table)
    gather_pairs(compositions, partners, table, parts, pair, 0, early)

    loads[2].wait()
    loads[3].wait()
    blend = 1.0 - jnp.exp(-rate[...])
    pick_rates(lists, blend, rates_out)
    rates_in[me] = rates_out[me]

    def rate_copy(source, d, target):
        return pltpu.make_async_remote_copy(
            src_ref=rates_out.at[d],
            dst_ref=rates_in.at[source],
            send_sem=rate_send.at[d],
            recv_sem=rate_recv.at[source],
            device_id=place(target),
            device_id_type=pl.DeviceIdType.MESH,
        )

    def send_rates(k, _):
        d = lax.rem(me + k, tiles)
        rate_copy(me, d, d).start()
        return 0


    loads[6].wait()
    for b in range(0, blocks, 4):
        hot1[:, b * LANES : (b + 4) * LANES] = hot_rows(row_block(slots, b // 4, 4 * LANES))
    for b in range(0, tiles, 4):
        hot2[:, b * LANES : (b + 4) * LANES] = hot_rows(row_block(lists, b // 4, 4 * LANES))
    loads[1].wait()
    inside(cells, diffusion, fields, rows_x, rows_y)
    gather_pairs(compositions, partners, table, parts, pair, early, soon)

    @pl.when(plane < planes - 1)
    def _():
        pl.semaphore_wait(late, tiles - (plane + 1) * PLANE)

    lax.fori_loop(1, tiles, send_rates, 0)

    def go_copy(source, d, target):
        return pltpu.make_async_remote_copy(
            src_ref=outgoing.at[d, 0:species],
            dst_ref=received.at[source, 0:species],
            send_sem=go_send.at[d],
            recv_sem=go_recv.at[source],
            device_id=place(target),
            device_id_type=pl.DeviceIdType.MESH,
        )

    def back_copy(source, d, target):
        return pltpu.make_async_remote_copy(
            src_ref=moments.at[d, 0 : species + 1],
            dst_ref=returned.at[source, 0 : species + 1],
            send_sem=back_send.at[d],
            recv_sem=back_recv.at[source],
            device_id=place(target),
            device_id_type=pl.DeviceIdType.MESH,
        )

    wide = acc1.shape[0] // ROWS
    sections = tiles // wide
    own = lax.div(me, wide)
    per_section = wide // PLANE

    def peer(section, k):
        turn = lax.div(k, PLANE)
        near = lax.rem(plane + 1 + turn, per_section)
        turn = jnp.where(section == own, near, turn)
        return section * wide + turn * PLANE + lax.rem(inner + k, PLANE)

    def fill(there):
        at = pl.ds(pl.multiple_of(there * (PLANE * LANES), PLANE * LANES), PLANE * LANES)
        hot = hot2[:, at]
        parts[0 : count // 2 * ROWS, :] = jnp.dot(
            field_table[...], jnp.concatenate([hot, hot], 0), preferred_element_type=F32
        )
        index = row_block(lists, there, PLANE * LANES)
        found = select_group(index, parts, count // 2)
        for i in range(PLANE):
            outgoing[there * PLANE + i] = found[:, i * LANES : (i + 1) * LANES]

    def send_go(there, first):
        def body(k, _):
            d = there * PLANE + lax.rem(inner + k, PLANE)
            go_copy(me, d, d).start()
            return 0

        lax.fori_loop(first, PLANE, body, 0)

    def far_plane(k):
        return lax.rem(own * per_section + k, planes)

    for i in range(4):

        @pl.when(receives[i])
        def _(i=i):
            halo_copy(i).wait_recv()

    rim(halo, diffusion, fields, blend, field_table, rows_x, rows_y)

    def go_far(k, _):
        fill(far_plane(k))
        send_go(far_plane(k), 0)
        return 0

    lax.fori_loop(per_section, planes - 1, go_far, 0)
    lax.fori_loop(planes - 1, planes, go_far, 0)
    gather_pairs(compositions, partners, table, parts, pair, soon, rounds)
    def go_near(k, _):
        there = own * per_section + lax.rem(plane + k, per_section)
        fill(there)
        send_go(there, 0)
        return 0

    lax.fori_loop(1, per_section, go_near, 0)
    fill(plane)
    received[me] = outgoing[me]
    send_go(plane, 1)
    loads[5].wait()

    def wait_rates(k, _):
        s = lax.rem(me + k, tiles)
        rate_copy(s, s, s).wait_recv()
        return 0

    lax.fori_loop(1, tiles, wait_rates, 0)
    spread_rates(slots, rates_in, rates)

    def weigh(b, _):
        at = pl.ds(pl.multiple_of(b * LANES, LANES), LANES)
        mine = compositions[:, at]
        fresh = mine - rates[pl.ds(b, 1), :] * mine - pair[0:species, at]
        new[:, at] = fresh
        weight = weights[pl.ds(b, 1), :]
        values = jnp.concatenate(
            [weight * fresh, weight, jnp.zeros((ROWS - species - 1, LANES), F32)], 0
        )
        top = values.astype(BF16)
        high[:, at] = top
        low[:, at] = (values - top.astype(F32)).astype(BF16)
        return 0

    lax.fori_loop(0, blocks, weigh, 0, unroll=4)

    per = left1.shape[1]

    def sum_slots(section):
        acc1[...] = jnp.zeros(acc1.shape, F32)

        def scatter(k, _):
            group = (row_block(slots, k, per) >> 8) - section * (wide // 2)
            cols = pl.ds(pl.multiple_of(k * per, per), per)
            scatter_block(
                group, hot1[:, cols], high[:, cols], low[:, cols], left1, acc1, wide // 2
            )
            return 0

        lax.fori_loop(0, blocks * LANES // per, scatter, 0)
        for i in range(wide):
            moments[section * wide + i] = acc_row(acc1, i)

    def send_back(section, first, last):
        def body(k, _):
            d = peer(section, k)
            back_copy(me, d, d).start()
            return 0

        lax.fori_loop(first, last, body, 0)

    def other(r, _):
        section = lax.rem(own + r, sections)
        sum_slots(section)
        send_back(section, 0, wide)
        return 0

    lax.fori_loop(1, sections, other, 0)

    sum_slots(own)
    send_back(own, 0, wide - PLANE)
    send_back(own, wide - PLANE + 1, wide)
    returned[me] = moments[me]

    def wait_go(s, _):
        go_copy(s, s, s).wait_recv()
        return 0

    def add_section(section):
        add_fields(received, slots, hot1, table, parts, new, section, wide // 2)

    lax.fori_loop(own * wide, me, wait_go, 0)
    lax.fori_loop(me + 1, (own + 1) * wide, wait_go, 0)
    add_section(own)
    acc2[...] = jnp.zeros(acc2.shape, F32)

    def wait_back(there, first, last):
        def body(i, _):
            s = there * PLANE + i
            back_copy(s, s, s).wait_recv()
            return 0

        lax.fori_loop(first, last, body, 0)

    def collect(there, first, many):
        at = [there * PLANE + first + i for i in range(many)]
        values = jnp.concatenate([returned[s] for s in at], 1)
        index = jnp.concatenate([lists[pl.ds(s, 1), :] for s in at], 1)
        top = values.astype(BF16)
        rest = (values - top.astype(F32)).astype(BF16)
        start = there * (PLANE * LANES) + first * LANES
        cols = pl.ds(pl.multiple_of(start, many * LANES), many * LANES)
        left = left2.at[:, 0 : many * LANES]
        scatter_block(index >> 8, hot2[:, cols], top, rest, left, acc2, count // 2)

    wait_back(plane, 0, inner)
    wait_back(plane, inner + 1, PLANE)
    collect(plane, 0, PLANE)
    near = own * per_section

    def collect_near(k, _):
        there = near + lax.rem(plane + k, per_section)
        wait_back(there, 0, PLANE)
        collect(there, 0, PLANE)
        return 0

    lax.fori_loop(1, per_section, collect_near, 0)
    def add_far(r, _):
        section = lax.rem(own + r, sections)
        lax.fori_loop(section * wide, (section + 1) * wide, wait_go, 0)
        add_section(section)
        return 0

    lax.fori_loop(1, sections, add_far, 0)

    for i in range(4):

        @pl.when(sends[i])
        def _(i=i):
            halo_copy(i).wait_send()

    def sent(k, _):
        d = lax.rem(me + k, tiles)
        rate_copy(me, d, d).wait_send()
        go_copy(me, d, d).wait_send()
        return 0

    lax.fori_loop(1, tiles, sent, 0)

    reverse = own < (sections + 1) // 2

    def far_back(k):
        return far_plane(jnp.where(reverse, planes - 1 + per_section - k, k))

    def collect_far(k, _):
        wait_back(far_back(k), 0, PLANE)
        collect(far_back(k), 0, PLANE)
        return 0

    lax.fori_loop(per_section, planes - 1, collect_far, 0)
    last = far_back(planes - 1)
    half = lax.div(lax.rem(inner + 1, PLANE), LAST)

    def finish(d, _):
        back_copy(me, d, d).wait_send()
        return 0

    def finish_plane(there):
        lax.fori_loop(there * PLANE, (there + 1) * PLANE, finish, 0)

    def finish_far(k, _):
        finish_plane(far_plane(k))
        return 0

    lax.fori_loop(per_section, planes - 1, finish_far, 0)
    lax.fori_loop(own * wide, me, finish, 0)
    lax.fori_loop(me + 1, (own + 1) * wide, finish, 0)
    for part in range(PLANE // LAST):
        first = lax.rem(half + 1 + part, PLANE // LAST) * LAST
        wait_back(last, first, first + LAST)
        collect(last, first, LAST)

    for j in range(count):
        total = acc_row(acc2, j)
        weight = total[species : species + 1]
        mean = total[:species] + fields[j, 0:species, :] * (blend[j : j + 1, :] * weight + 1.0)
        out[pl.ds(j, species, stride=count), :] = mean * (1.0 / (weight + 1.0))

    finish_plane(far_plane(planes - 1))


def hand_over(first, second, first_out, second_out, sems):
    copies = [
        pltpu.make_async_copy(first, first_out, sems.at[0]),
        pltpu.make_async_copy(second, second_out, sems.at[1]),
    ]
    for copy in copies:
        copy.start()
    for copy in copies:
        copy.wait()


def on_device(
    cell_means, diffusion, mix_rate, send_lists, compositions, weights, particle_slots, partners
):
    species, rows_x, rows_y, depth = cell_means.shape
    count = rows_x * rows_y
    tiles = send_lists.shape[1]
    particles = compositions.shape[1]
    blocks = particles // LANES
    vmem = lambda *shape: pltpu.VMEM(shape, F32)
    half_vmem = lambda *shape: pltpu.VMEM(shape, BF16)
    operands = (
        cell_means.reshape(species * count, depth),
        diffusion.reshape(count, depth),
        mix_rate.reshape(count, depth),
        send_lists[0],
        compositions,
        weights.reshape(blocks, LANES),
        particle_slots.reshape(blocks, LANES),
        partners.reshape(blocks, LANES),
    )
    out, new = pl.pallas_call(
        functools.partial(
            whole_kernel, lax.axis_size("gx"), lax.axis_size("gy"), rows_x, rows_y
        ),
        out_shape=(
            pltpu.VMEM((species * count, LANES), F32),
            pltpu.VMEM((species, particles), F32),
        ),
        in_specs=[pl.BlockSpec(memory_space=pltpu.HBM)] * 8,
        out_specs=[pl.BlockSpec(memory_space=pltpu.VMEM)] * 2,
        name="whole_kernel",
        scratch_shapes=[pltpu.VMEM(a.shape, a.dtype) for a in operands]
        + [
            vmem(rows_x, rows_y, ROWS, LANES),
            vmem(4, max(rows_x, rows_y), ROWS, LANES),
            vmem(count, ROWS, LANES),
            vmem(tiles, 1, LANES),
            vmem(tiles, 1, LANES),
            vmem(blocks, LANES),
            vmem(tiles, ROWS, LANES),
            vmem(tiles, ROWS, LANES),
            vmem(tiles, ROWS, LANES),
            vmem(tiles, ROWS, LANES),
            half_vmem(particles // 256 * ROWS, 512),
            vmem(particles // 256 * ROWS, WIDE),
            vmem(ROWS, particles),
            half_vmem(ROWS, particles),
            half_vmem(ROWS, particles),
            half_vmem(256, particles),
            half_vmem(256, tiles * LANES),
            half_vmem(2 * PLANE * ROWS, 1024),
            vmem(2 * PLANE * ROWS, 256),
            half_vmem(count // 2 * ROWS, 512),
            half_vmem(count * ROWS, PLANE * LANES),
            vmem(count * ROWS, 256),
            pltpu.SemaphoreType.DMA((8,)),
            pltpu.SemaphoreType.DMA((4,)),
            pltpu.SemaphoreType.DMA((4,)),
            pltpu.SemaphoreType.DMA((tiles,)),
            pltpu.SemaphoreType.DMA((tiles,)),
            pltpu.SemaphoreType.DMA((tiles,)),
            pltpu.SemaphoreType.DMA((tiles,)),
            pltpu.SemaphoreType.DMA((tiles,)),
            pltpu.SemaphoreType.DMA((tiles,)),
            pltpu.SemaphoreType.REGULAR,
        ],
        compiler_params=pltpu.CompilerParams(
            collective_id=0, has_side_effects=True, vmem_limit_bytes=63 * 1024 * 1024
        ),
    )(*operands)
    out, new = pl.pallas_call(
        hand_over,
        out_shape=tuple(jax.ShapeDtypeStruct(a.shape, a.dtype) for a in (out, new)),
        in_specs=[pl.BlockSpec(memory_space=pltpu.VMEM)] * 2,
        out_specs=[pl.BlockSpec(memory_space=pltpu.HBM)] * 2,
        scratch_shapes=[pltpu.SemaphoreType.DMA((2,))],
        compiler_params=pltpu.CompilerParams(vmem_limit_bytes=1024 * 1024),
        name="hand_over",
    )(out, new)
    return out.reshape(species, rows_x, rows_y, depth), new


def solution(mesh):
    in_specs = (
        P(None, "gx", "gy", None),
        P("gx", "gy", None),
        P("gx", "gy", None),
        P(("gx", "gy"), None, None),
        P(None, ("gx", "gy")),
        P(("gx", "gy")),
        P(("gx", "gy")),
        P(("gx", "gy")),
    )
    out_specs = (P(None, "gx", "gy", None), P(None, ("gx", "gy")))
    return jax.shard_map(
        on_device, mesh=mesh, in_specs=in_specs, out_specs=out_specs, check_vma=False
    )
```
